32 devices in a mesh: rep: 4 (over y, x), fsdp: 8 (over z, core).
Axes of the slice: x: 2, y: 2, z: 4, core: 2. Of those that a mesh axis runs over, the one named last changes fastest.
Arguments:
- tokens: bfloat16 [64, 128, 2048], P(('rep', 'fsdp')), may hold values from -6 to 6
- lengths: int32 [64], P(('rep', 'fsdp')), may hold values from 1 to 128, 6144 in all
- cotangent: bfloat16 [64, 128, 2048], P(('rep', 'fsdp')), may hold values from -6 to 6
- qkv_weight: bfloat16 [2048, 6144], P('fsdp'), may hold values from -0.125 to 0.125
- qv_bias: bfloat16 [4096], P('fsdp'), may hold values from -3 to 3
- out_weight: bfloat16 [2048, 2048], P('fsdp'), may hold values from -0.5 to 0.5
- out_bias: bfloat16 [2048], P('fsdp'), may hold values from -3 to 3
- attn_gain: bfloat16 [2048], P('fsdp'), may hold values from 0.5 to 1.5
- attn_shift: bfloat16 [2048], P('fsdp'), may hold values from -3 to 3
- up_weight: bfloat16 [2048, 8192], P('fsdp'), may hold values from -0.125 to 0.125
- up_bias: bfloat16 [8192], P('fsdp'), may hold values from -3 to 3
- down_weight: bfloat16 [8192, 2048], P('fsdp'), may hold values from -0.0625 to 0.0625
- down_bias: bfloat16 [2048], P('fsdp'), may hold values from -3 to 3
- ffn_gain: bfloat16 [2048], P('fsdp'), may hold values from 0.5 to 1.5
- ffn_shift: bfloat16 [2048], P('fsdp'), may hold values from -3 to 3
Outputs:
- output: bfloat16 [64, 128, 2048], P(('rep', 'fsdp'))
- input_grad: float32 [64, 128, 2048], P(('rep', 'fsdp'))
- qkv_weight_grad: float32 [2048, 6144], P('fsdp')
- qv_bias_grad: float32 [4096], P('fsdp')
- out_weight_grad: float32 [2048, 2048], P('fsdp')
- out_bias_grad: float32 [2048], P('fsdp')
- attn_gain_grad: float32 [2048], P('fsdp')
- attn_shift_grad: float32 [2048], P('fsdp')
- up_weight_grad: float32 [2048, 8192], P('fsdp')
- up_bias_grad: float32 [8192], P('fsdp')
- down_weight_grad: float32 [8192, 2048], P('fsdp')
- down_bias_grad: float32 [2048], P('fsdp')
- ffn_gain_grad: float32 [2048], P('fsdp')
- ffn_shift_grad: float32 [2048], P('fsdp')
The draws below stay inside these ranges and needn't reach their ends.
Inputs may be any that keep to these rules, and one draw needn't show every extreme that they name: Slot i holds lengths[i] real tokens followed by padding; some slot is full.
All inputs are finite; a program needn't handle non-finite values. No bound on the sum of `lengths` on one device may be relied on, other than what follows from the above.
Results may differ from the reference program's by a relative error of at most 0.02.
Values may be sent and summed in bfloat16 or wider, within the bound.
No kernel may reach another device: no remote copies, remote signals or barrier semaphores. Data moves between devices by JAX's collectives and lax.ppermute only.
A program may use at most 576 MiB of HBM per device.

```python
import math
import jax
import jax.numpy as jnp
import numpy as np
from jax import lax

D = 2048
HEADS = 16
HEAD_DIM = 128
FF = 8192
SEQ = 128
SEQS = 64


def steps_of(rng, shape, shards, low, high):
    level, own = 1.0, jax.random.fold_in(rng, 6)
    for axis_at, shards_of in shards:
        heights = jnp.exp(jax.random.uniform(jax.random.fold_in(own, axis_at), (shards_of,), jnp.float32, low / len(shards), high / len(shards)))
        level = level * jnp.repeat(heights, shape[axis_at] // shards_of).reshape([-1 if axis == axis_at else 1 for axis in range(len(shape))])
    return level


def length_profile(count, total, limit, skew):
    loads = [(1 << 20) // math.isqrt(standing ** skew) + 1 for standing in range(2, count + 1)]
    surplus, given = total - limit - (count - 1), [1] * (count - 1)
    while surplus > 0:
        free = [i for i in range(count - 1) if given[i] < limit]
        mass, remaining = sum([loads[i] for i in free]), surplus
        for i in free:
            more = min(limit - given[i], max(1, remaining * loads[i] // mass), surplus)
            given[i] = given[i] + more
            surplus = surplus - more
    return np.array([limit] + given)


def uneven(key, count, total, reach, slope):
    if count == 2:
        one = jax.random.randint(key, (), max(1, total - reach), min(reach, total - 1) + 1)
        return jnp.stack([one, total - one])
    sizes = jnp.asarray(length_profile(count, total, reach, slope), jnp.int32)
    pairs = (count - 1) // 2
    source_of, taker = sizes[1:1 + 2 * pairs:2], sizes[2:2 + 2 * pairs:2]
    slack = jnp.minimum(source_of - 1, reach - taker)
    passed = jax.random.randint(jax.random.fold_in(key, 1), (pairs,), 0, 1 << 20) % (slack + 1)
    sizes = sizes.at[1:1 + 2 * pairs:2].set(source_of - passed).at[2:2 + 2 * pairs:2].set(taker + passed)
    return sizes[jax.random.permutation(jax.random.fold_in(key, 2), count)]


def centred(rng, shape, width, bound, shards=(), kind=jnp.bfloat16):
    values = jax.random.normal(rng, shape, jnp.float32) * width
    if len(shards) > 0:
        values = steps_of(rng, shape, shards, -0.22, 0.18) * values
    return jnp.clip(values, min=-bound, max=bound).astype(kind)


def setup_inputs(seed: int = 0) -> dict:
    streams_of = jax.random.split(jax.random.key(seed), 16)
    return {
        "tokens": centred(streams_of[0], (SEQS, SEQ, D), 1.0, 6.0, ((0, 32),)),
        "lengths": uneven(streams_of[1], SEQS, SEQS * SEQ * 3 // 4, SEQ, 1).astype(jnp.int32),
        "cotangent": centred(streams_of[2], (SEQS, SEQ, D), 1.0, 6.0, ((0, 32),)),
        "qkv_weight": centred(streams_of[3], (D, 3 * D), D ** -0.5, 0.125, ((0, 8),)),
        "qv_bias": centred(streams_of[4], (2 * D,), 0.5, 3.0, ((0, 8),)),
        "out_weight": centred(streams_of[5], (D, D), (D // 16) ** -0.5, 0.5, ((0, 8),)),
        "out_bias": centred(streams_of[6], (D,), 0.5, 3.0, ((0, 8),)),
        "attn_gain": jnp.clip(1.0 + 0.1 * jax.random.normal(streams_of[7], (D,), jnp.float32), 0.5, 1.5).astype(jnp.bfloat16),
        "attn_shift": centred(streams_of[8], (D,), 0.5, 3.0, ((0, 8),)),
        "up_weight": centred(streams_of[9], (D, FF), D ** -0.5, 0.125, ((0, 8),)),
        "up_bias": centred(streams_of[10], (FF,), 0.5, 3.0, ((0, 8),)),
        "down_weight": centred(streams_of[11], (FF, D), FF ** -0.5, 0.0625, ((0, 8),)),
        "down_bias": centred(streams_of[12], (D,), 0.5, 3.0, ((0, 8),)),
        "ffn_gain": jnp.clip(1.0 + 0.1 * jax.random.normal(streams_of[13], (D,), jnp.float32), 0.5, 1.5).astype(jnp.bfloat16),
        "ffn_shift": centred(streams_of[14], (D,), 0.5, 3.0, ((0, 8),)),
    }


@jax.custom_vjp
def low(v):
    return lax.optimization_barrier(v.astype(jnp.bfloat16)).astype(jnp.float32)

@jax.custom_vjp
def low_back(v):
    return v

def low_keep(v):
    return (low(v), None)

def low_pass(kept, grad):
    return (grad,)

def back_keep(v):
    return (v, None)

def back_low(kept, grad):
    return (low(grad),)
low.defvjp(low_keep, low_pass)
low_back.defvjp(back_keep, back_low)
eps_norm = 1e-05

def layer_norm(resid, gain, shift):
    center = resid - lax.optimization_barrier(jnp.mean(resid, -1, keepdims=True))
    spread = lax.optimization_barrier(jnp.mean(center * center, -1, keepdims=True))
    return center * lax.rsqrt(spread + eps_norm) * gain + shift

def forward(params, inputs, valid):
    qkv_weight, qv_bias, out_weight, out_bias, attn_gain, attn_shift, up_weight, up_bias, down_weight, down_bias, ffn_gain, ffn_shift = params
    highest = lax.Precision.HIGHEST
    groups = inputs.shape[0]
    flat = inputs.reshape(-1, D)
    qkv = jnp.dot(flat, qkv_weight, precision=highest)
    query = low(low_back(qkv[:, :D] + qv_bias[:D]))
    keys = low(low_back(qkv[:, D:2 * D]))
    values = low(low_back(qkv[:, 2 * D:] + qv_bias[D:]))
    query = query.reshape(groups, SEQ, HEADS, HEAD_DIM)
    keys = keys.reshape(groups, SEQ, HEADS, HEAD_DIM)
    values = values.reshape(groups, SEQ, HEADS, HEAD_DIM)
    raw = jnp.einsum('gqhd,gkhd->ghqk', query, keys, precision=highest)
    scores = low_back(raw * HEAD_DIM ** (-0.5))
    scores = jnp.where(valid[:, None, None, :], scores, -1000000000.0)
    probs = jax.nn.softmax(scores, axis=-1)
    mixed = jnp.einsum('ghqk,gkhd->gqhd', low(probs), values, precision=highest)
    mixed = low(low_back(mixed.reshape(-1, D)))
    attn = low_back(jnp.dot(mixed, out_weight, precision=highest) + out_bias)
    first = layer_norm(flat + attn, attn_gain, attn_shift)
    hidden = low_back(jnp.dot(low(first), up_weight, precision=highest) + up_bias)
    active = low(jax.nn.gelu(hidden, approximate=True))
    branch = low_back(jnp.dot(active, down_weight, precision=highest) + down_bias)
    result = layer_norm(first + branch, ffn_gain, ffn_shift)
    return result.reshape(groups, SEQ, D)

def reference(tokens, lengths, cotangent, qkv_weight, qv_bias, out_weight, out_bias, attn_gain, attn_shift, up_weight, up_bias, down_weight, down_bias, ffn_gain, ffn_shift):
    params = tuple((w.astype(jnp.float32) for w in (qkv_weight, qv_bias, out_weight, out_bias, attn_gain, attn_shift, up_weight, up_bias, down_weight, down_bias, ffn_gain, ffn_shift)))
    group = math.gcd(SEQS, max(1, 4096 // SEQ))
    steps_total = SEQS // group
    inputs = tokens.astype(jnp.float32).reshape(steps_total, group, SEQ, D)
    grads_in = cotangent.astype(jnp.float32).reshape(steps_total, group, SEQ, D)
    counts = lengths.astype(jnp.int32).reshape(steps_total, group)
    positions = jnp.arange(SEQ).astype(jnp.int32)

    def step(totals, item):
        block, count, grad_out = item
        valid = positions[None, :] < count[:, None]
        result, back = jax.vjp(lambda prm, xin: forward(prm, xin, valid), params, block)
        masked = grad_out * valid[..., None].astype(jnp.float32)
        grad_params, grad_input = back(masked)
        totals = jax.tree.map(lambda a, b: a + b, totals, grad_params)
        return (totals, (result, grad_input))
    start = jax.tree.map(jnp.zeros_like, params)
    totals, (results, input_grads) = lax.scan(step, start, (inputs, counts, grads_in))
    output = results.reshape(SEQS, SEQ, D).astype(jnp.bfloat16)
    input_grad = input_grads.reshape(SEQS, SEQ, D)
    return (output, input_grad, totals[0], totals[1], totals[2], totals[3], totals[4], totals[5], totals[6], totals[7], totals[8], totals[9], totals[10], totals[11])
```

```python
import jax
import jax.numpy as jnp
from jax import lax
from jax.experimental import pallas as pl
from jax.experimental.pallas import tpu as pltpu
from jax.sharding import PartitionSpec as P

D = 2048
HEADS = 16
HEAD_DIM = 128
EPS = 1e-05
BF = jnp.bfloat16
F32 = jnp.float32


def mm(a, b):
    return jnp.dot(a, b, preferred_element_type=F32)


def mm_nt(a, b):
    return lax.dot_general(a, b, (((1,), (1,)), ((), ())), preferred_element_type=F32)


def mm_tn(a, b):
    return lax.dot_general(a, b, (((0,), (0,)), ((), ())), preferred_element_type=F32)


def head_probs(q, k, length, factor):
    s = mm_nt(q, k) * factor
    cols = lax.broadcasted_iota(jnp.int32, s.shape, 1)
    s = jnp.where(cols < length, s, -1000000000.0)
    e = jnp.exp(s - jnp.max(s, -1, keepdims=True))
    return e / jnp.sum(e, -1, keepdims=True)


def attn_fwd_kernel(len_ref, qkv_ref, o_ref):
    width = o_ref.shape[1]
    length = len_ref[pl.program_id(0)]
    for h in range(width // HEAD_DIM):
        at = h * HEAD_DIM
        q = qkv_ref[:, at : at + HEAD_DIM]
        k = qkv_ref[:, width + at : width + at + HEAD_DIM]
        v = qkv_ref[:, 2 * width + at : 2 * width + at + HEAD_DIM]
        p = head_probs(q, k, length, HEAD_DIM**-0.5).astype(BF)
        o_ref[:, at : at + HEAD_DIM] = mm(p, v).astype(BF)


def attn_bwd_kernel(len_ref, qkv_ref, do_ref, dqkv_ref, sums_ref):
    width = do_ref.shape[1]
    factor = HEAD_DIM**-0.5
    length = len_ref[pl.program_id(0)]

    @pl.when(pl.program_id(0) == 0)
    def _():
        sums_ref[...] = jnp.zeros_like(sums_ref)

    for h in range(width // HEAD_DIM):
        at = h * HEAD_DIM
        q = qkv_ref[:, at : at + HEAD_DIM]
        k = qkv_ref[:, width + at : width + at + HEAD_DIM]
        v = qkv_ref[:, 2 * width + at : 2 * width + at + HEAD_DIM]
        do = do_ref[:, at : at + HEAD_DIM]
        p = head_probs(q, k, length, factor)
        dp = mm_nt(do, v)
        dv = mm_tn(p.astype(BF), do).astype(BF)
        ds = (p * (dp - jnp.sum(p * dp, -1, keepdims=True))).astype(BF)
        dq = (mm(ds, k) * factor).astype(BF)
        dk = (mm_tn(ds, q) * factor).astype(BF)
        for part, grad in ((0, dq), (1, dk), (2, dv)):
            cols = slice(part * width + at, part * width + at + HEAD_DIM)
            dqkv_ref[:, cols] = grad
            sums_ref[:, cols] += jnp.sum(grad.astype(F32), 0, keepdims=True)


def attn_fwd(lengths, qkv, seq):
    rows, wide = qkv.shape
    width = wide // 3
    return pl.pallas_call(
        attn_fwd_kernel,
        grid_spec=pltpu.PrefetchScalarGridSpec(
            num_scalar_prefetch=1,
            grid=(rows // seq,),
            in_specs=[pl.BlockSpec((seq, wide), lambda i, n: (i, 0))],
            out_specs=pl.BlockSpec((seq, width), lambda i, n: (i, 0)),
        ),
        out_shape=jax.ShapeDtypeStruct((rows, width), BF),
        cost_estimate=pl.CostEstimate(
            flops=4 * rows * seq * width, bytes_accessed=8 * rows * width, transcendentals=rows * seq * width // HEAD_DIM
        ),
    )(lengths, qkv)


def attn_bwd(lengths, qkv, do, seq):
    rows, wide = qkv.shape
    width = wide // 3
    return pl.pallas_call(
        attn_bwd_kernel,
        grid_spec=pltpu.PrefetchScalarGridSpec(
            num_scalar_prefetch=1,
            grid=(rows // seq,),
            in_specs=[
                pl.BlockSpec((seq, wide), lambda i, n: (i, 0)),
                pl.BlockSpec((seq, width), lambda i, n: (i, 0)),
            ],
            out_specs=[
                pl.BlockSpec((seq, wide), lambda i, n: (i, 0)),
                pl.BlockSpec((1, wide), lambda i, n: (0, 0)),
            ],
        ),
        out_shape=[jax.ShapeDtypeStruct((rows, wide), BF), jax.ShapeDtypeStruct((1, wide), F32)],
        cost_estimate=pl.CostEstimate(
            flops=10 * rows * seq * width, bytes_accessed=14 * rows * width, transcendentals=rows * seq * width // HEAD_DIM
        ),
    )(lengths, qkv, do)


def norm_forward(resid, gain, shift):
    center = resid - jnp.mean(resid, -1, keepdims=True)
    inv = lax.rsqrt(jnp.mean(center * center, -1, keepdims=True) + EPS)
    n = center * inv
    return n * gain + shift, n, inv


def norm_backward(g, gain, n, inv):
    dn = g * gain
    d = inv * (dn - jnp.mean(dn, -1, keepdims=True) - n * jnp.mean(dn * n, -1, keepdims=True))
    return d, jnp.sum(g * n, 0), jnp.sum(g, 0)


class Moves:
    def __init__(self, reps, shards):
        self.reps, self.shards = reps, shards
        self.square = reps == 4
        self.me = lax.axis_index("rep")
        self.xs = [(r, r ^ 1) for r in range(reps)]
        self.ys = [(r, r ^ 2) for r in range(reps)]
        self.ds = [(r, r ^ 3) for r in range(reps)]

    def over_x(self, a):
        return lax.ppermute(a, "rep", self.xs)

    def over_y(self, a):
        return lax.ppermute(a, "rep", self.ys)

    def owner(self, k):
        return self.me ^ k if self.square else k

    def gather_blocks(self, a):
        if not self.square:
            whole = lax.all_gather(a, "rep", axis=0, tiled=False)
            return [whole[k] for k in range(self.reps)]
        half = a.shape[0] // 2
        ax, ay = self.over_x(a), self.over_y(a)
        low, high = self.over_x(ay[:half]), self.over_y(ax[half:])
        return [a, ax, ay, jnp.concatenate([low, high], 0)]

    def gather_small(self, a):
        if not self.square:
            return lax.all_gather(a, "rep", axis=0, tiled=True)
        return jnp.concatenate([a, self.over_x(a), self.over_y(a), lax.ppermute(a, "rep", self.ds)], 0)

    def scatter_sum(self, part):
        if not self.square:
            whole = jnp.concatenate([part(k).astype(BF) for k in range(self.reps)], 0)
            return lax.psum_scatter(whole, "rep", scatter_dimension=0, tiled=True).astype(F32)
        d = part(3).astype(BF)
        half = d.shape[0] // 2
        for_y, for_x = self.over_x(d[:half]), self.over_y(d[half:])
        px, py = part(1), part(2)
        px = jnp.concatenate([px[:half], px[half:] + for_x.astype(F32)], 0).astype(BF)
        py = jnp.concatenate([py[:half] + for_y.astype(F32), py[half:]], 0).astype(BF)
        got_x, got_y = self.over_x(px), self.over_y(py)
        return part(0) + got_x.astype(F32) + got_y.astype(F32)

    def swap(self, a):
        return lax.all_to_all(a, "rep", 0, 0, tiled=True)

    def gather_weight(self, w):
        return lax.all_gather(w, "fsdp", axis=0, tiled=True)

    def scatter_weight(self, g):
        return lax.psum_scatter(g, "fsdp", scatter_dimension=0, tiled=True)


def per_device(
    tokens,
    lengths,
    cotangent,
    qkv_weight,
    qv_bias,
    out_weight,
    out_bias,
    attn_gain,
    attn_shift,
    up_weight,
    up_bias,
    down_weight,
    down_bias,
    ffn_gain,
    ffn_shift,
    reps,
    shards,
):
    mv = Moves(reps, shards)
    r = mv.me
    slots, seq, _ = tokens.shape
    rows = slots * seq
    ff = up_weight.shape[1]
    dr, fr = D // reps, ff // reps
    fpart = ff // (shards * reps)
    wrows = qkv_weight.shape[0]

    small = [qv_bias, out_bias, attn_gain, attn_shift, up_bias, down_bias, ffn_gain, ffn_shift]
    sizes = [s.shape[0] for s in small]
    packed = lax.all_gather(jnp.concatenate(small, 0), "fsdp", axis=0, tiled=False).astype(F32)
    full, at = [], 0
    for size in sizes:
        full.append(packed[:, at : at + size].reshape(-1))
        at += size
    b_qv, b_out, g_attn, s_attn, b_up, b_down, g_ffn, s_ffn = full
    bias_q = lax.dynamic_slice(b_qv, (r * dr,), (dr,))
    bias_v = lax.dynamic_slice(b_qv, (D + r * dr,), (dr,))
    bias_qkv = jnp.concatenate([bias_q, jnp.zeros_like(bias_q), bias_v], 0)
    bias_up = lax.dynamic_index_in_dim(b_up.reshape(shards, reps, fpart), r, 1, False).reshape(-1)

    qkv_own = lax.dynamic_index_in_dim(qkv_weight.reshape(wrows, 3, reps, dr), r, 2, False).reshape(wrows, 3 * dr)
    out_own = lax.dynamic_slice(out_weight, (0, r * dr), (wrows, dr))
    up_own = lax.dynamic_index_in_dim(up_weight.reshape(wrows, shards, reps, fpart), r, 2, False).reshape(wrows, fr)
    down_own = lax.dynamic_slice(down_weight, (r * fpart, 0), (fpart, D))
    w_qkv = mv.gather_weight(qkv_own)
    w_out_cols = mv.gather_weight(out_own)
    w_out = mv.swap(w_out_cols)
    w_out = w_out.reshape(reps, dr, dr).transpose(1, 0, 2).reshape(dr, D)
    w_up = mv.gather_weight(up_own)
    w_down = mv.gather_weight(down_own)

    x = tokens.reshape(rows, D)
    lens = mv.gather_small(lengths)
    x_all = jnp.concatenate(mv.gather_blocks(x), 0)
    qkv = (mm(x_all, w_qkv) + bias_qkv).astype(BF)
    o = attn_fwd(lens, qkv, seq)
    block = lambda a, k: a[k * rows : (k + 1) * rows]
    attn = mv.scatter_sum(lambda k: mm(block(o, k), w_out))
    x1, n1, inv1 = norm_forward(x.astype(F32) + attn + b_out, g_attn, s_attn)

    x1_all = jnp.concatenate(mv.gather_blocks(x1.astype(BF)), 0)
    hidden = mm(x1_all, w_up) + bias_up
    act, gelu_back = jax.vjp(lambda h: jax.nn.gelu(h, approximate=True), hidden)
    act = act.astype(BF)
    branch = mv.scatter_sum(lambda k: mm(block(act, k), w_down))
    result, n2, inv2 = norm_forward(x1 + branch + b_down, g_ffn, s_ffn)
    output = result.astype(BF).reshape(slots, seq, D)

    valid = (jnp.arange(seq, dtype=jnp.int32)[None, :] < lengths[:, None]).astype(F32)
    g = cotangent.reshape(rows, D).astype(F32) * valid.reshape(rows, 1)
    dr2, d_gffn, d_sffn = norm_backward(g, g_ffn, n2, inv2)
    df = dr2.astype(BF)
    df_all = jnp.concatenate(mv.gather_blocks(df), 0)
    d_wdown = mv.scatter_weight(mm_tn(act, df_all).astype(BF))
    d_bdown = jnp.sum(df.astype(F32), 0)
    (dh,) = gelu_back(mm_nt(df_all, w_down))
    dh = dh.astype(BF)
    d_wup = mv.scatter_weight(mm_tn(x1_all, dh).astype(BF))
    d_bup = jnp.sum(dh.astype(F32), 0)
    dx1 = dr2 + mv.scatter_sum(lambda k: mm_nt(block(dh, k), w_up))

    dr1, d_gattn, d_sattn = norm_backward(dx1, g_attn, n1, inv1)
    dt = dr1.astype(BF)
    dt_all = jnp.concatenate(mv.gather_blocks(dt), 0)
    d_bout = jnp.sum(dt.astype(F32), 0)
    d_wout = mm_tn(o, dt_all).astype(BF)
    d_wout = mv.swap(d_wout.reshape(dr, reps, dr).transpose(1, 0, 2).reshape(reps * dr, dr))
    d_wout = mv.scatter_weight(d_wout)
    do = mm_nt(dt_all, w_out).astype(BF)
    dqkv, sums = attn_bwd(lens, qkv, do, seq)
    d_wqkv = mv.scatter_weight(mm_tn(x_all, dqkv).astype(BF))
    input_grad = dr1 + mv.scatter_sum(lambda k: mm_nt(block(dqkv, k), w_qkv))
    input_grad = input_grad.reshape(slots, seq, D)

    def spread(shard, shape, at):
        total = jnp.zeros(shape, F32)
        for k, piece in enumerate(mv.gather_blocks(shard)):
            start = [0] * len(shape)
            start[at] = mv.owner(k)
            kept = list(shape)
            kept[at] = 1
            total = lax.dynamic_update_slice(total, piece.astype(F32).reshape(kept), start)
        return total

    d_wdown = spread(d_wdown, (reps, fpart, D), 0).reshape(down_weight.shape)
    d_wup = spread(d_wup, (wrows, shards, reps, fpart), 2).reshape(up_weight.shape)
    d_wout = spread(d_wout, (wrows, reps, dr), 1).reshape(out_weight.shape)
    d_wqkv = spread(d_wqkv, (wrows, 3, reps, dr), 2).reshape(qkv_weight.shape)

    zero = jnp.zeros((2, D), F32)
    d_qv = lax.dynamic_update_slice(zero, jnp.stack([sums[0, :dr], sums[0, 2 * dr :]]), (0, r * dr)).reshape(-1)
    d_bup = lax.dynamic_update_slice(
        jnp.zeros((shards, reps, fpart), F32), d_bup.reshape(shards, 1, fpart), (0, r, 0)
    ).reshape(-1)
    grads = [d_qv, d_bout, d_gattn, d_sattn, d_bup, d_bdown, d_gffn, d_sffn]
    packed = jnp.concatenate([v.reshape(shards, -1) for v in grads], 1)
    packed = lax.psum(packed, ("rep", "fsdp"))
    packed = lax.dynamic_index_in_dim(packed, lax.axis_index("fsdp"), 0, False)
    pieces, at = [], 0
    for size in sizes:
        pieces.append(packed[at : at + size])
        at += size
    d_qv, d_bout, d_gattn, d_sattn, d_bup, d_bdown, d_gffn, d_sffn = pieces
    return (
        output,
        input_grad,
        d_wqkv,
        d_qv,
        d_wout,
        d_bout,
        d_gattn,
        d_sattn,
        d_wup,
        d_bup,
        d_wdown,
        d_bdown,
        d_gffn,
        d_sffn,
    )


def solution(mesh):
    reps, shards = mesh.shape["rep"], mesh.shape["fsdp"]
    seqs = P(("rep", "fsdp"), None, None)
    mat, vec = P("fsdp", None), P("fsdp")

    def program(*args):
        return per_device(*args, reps=reps, shards=shards)

    params = (mat, vec, mat, vec, vec, vec, mat, vec, mat, vec, vec, vec)
    return jax.shard_map(
        program,
        mesh=mesh,
        in_specs=(seqs, P(("rep", "fsdp")), seqs) + params,
        out_specs=(seqs, seqs) + params,
        check_vma=False,
    )
```

```python
import jax
import jax.numpy as jnp
from jax import lax
from jax.experimental import pallas as pl
from jax.experimental.pallas import tpu as pltpu
from jax.sharding import PartitionSpec as P

D = 2048
HEADS = 16
HEAD_DIM = 128
EPS = 1e-05
BF = jnp.bfloat16
F32 = jnp.float32


def mm(a, b):
    return jnp.dot(a, b, preferred_element_type=F32)


def mm_nt(a, b):
    return lax.dot_general(a, b, (((1,), (1,)), ((), ())), preferred_element_type=F32)


def mm_tn(a, b):
    return lax.dot_general(a, b, (((0,), (0,)), ((), ())), preferred_element_type=F32)


def head_probs(q, k, length, factor):
    s = mm_nt(q, k) * factor
    cols = lax.broadcasted_iota(jnp.int32, s.shape, 1)
    s = jnp.where(cols < length, s, -1000000000.0)
    e = jnp.exp(s - jnp.max(s, -1, keepdims=True))
    return e / jnp.sum(e, -1, keepdims=True)


def attn_fwd_kernel(len_ref, qkv_ref, o_ref):
    width = o_ref.shape[1]
    length = len_ref[pl.program_id(0)]
    for h in range(width // HEAD_DIM):
        at = h * HEAD_DIM
        q = qkv_ref[:, at : at + HEAD_DIM]
        k = qkv_ref[:, width + at : width + at + HEAD_DIM]
        v = qkv_ref[:, 2 * width + at : 2 * width + at + HEAD_DIM]
        p = head_probs(q, k, length, HEAD_DIM**-0.5).astype(BF)
        o_ref[:, at : at + HEAD_DIM] = mm(p, v).astype(BF)


def attn_bwd_kernel(len_ref, qkv_ref, do_ref, dqkv_ref, sums_ref):
    width = do_ref.shape[1]
    factor = HEAD_DIM**-0.5
    length = len_ref[pl.program_id(0)]

    @pl.when(pl.program_id(0) == 0)
    def _():
        sums_ref[...] = jnp.zeros_like(sums_ref)

    for h in range(width // HEAD_DIM):
        at = h * HEAD_DIM
        q = qkv_ref[:, at : at + HEAD_DIM]
        k = qkv_ref[:, width + at : width + at + HEAD_DIM]
        v = qkv_ref[:, 2 * width + at : 2 * width + at + HEAD_DIM]
        do = do_ref[:, at : at + HEAD_DIM]
        p = head_probs(q, k, length, factor)
        dp = mm_nt(do, v)
        dv = mm_tn(p.astype(BF), do).astype(BF)
        ds = (p * (dp - jnp.sum(p * dp, -1, keepdims=True))).astype(BF)
        dq = (mm(ds, k) * factor).astype(BF)
        dk = (mm_tn(ds, q) * factor).astype(BF)
        for part, grad in ((0, dq), (1, dk), (2, dv)):
            cols = slice(part * width + at, part * width + at + HEAD_DIM)
            dqkv_ref[:, cols] = grad
            sums_ref[:, cols] += jnp.sum(grad.astype(F32), 0, keepdims=True)


def attn_fwd(lengths, qkv, seq):
    rows, wide = qkv.shape
    width = wide // 3
    return pl.pallas_call(
        attn_fwd_kernel,
        grid_spec=pltpu.PrefetchScalarGridSpec(
            num_scalar_prefetch=1,
            grid=(rows // seq,),
            in_specs=[pl.BlockSpec((seq, wide), lambda i, n: (i, 0))],
            out_specs=pl.BlockSpec((seq, width), lambda i, n: (i, 0)),
        ),
        out_shape=jax.ShapeDtypeStruct((rows, width), BF),
        cost_estimate=pl.CostEstimate(
            flops=4 * rows * seq * width, bytes_accessed=8 * rows * width, transcendentals=rows * seq * width // HEAD_DIM
        ),
    )(lengths, qkv)


def attn_bwd(lengths, qkv, do, seq):
    rows, wide = qkv.shape
    width = wide // 3
    return pl.pallas_call(
        attn_bwd_kernel,
        grid_spec=pltpu.PrefetchScalarGridSpec(
            num_scalar_prefetch=1,
            grid=(rows // seq,),
            in_specs=[
                pl.BlockSpec((seq, wide), lambda i, n: (i, 0)),
                pl.BlockSpec((seq, width), lambda i, n: (i, 0)),
            ],
            out_specs=[
                pl.BlockSpec((seq, wide), lambda i, n: (i, 0)),
                pl.BlockSpec((1, wide), lambda i, n: (0, 0)),
            ],
        ),
        out_shape=[jax.ShapeDtypeStruct((rows, wide), BF), jax.ShapeDtypeStruct((1, wide), F32)],
        cost_estimate=pl.CostEstimate(
            flops=10 * rows * seq * width, bytes_accessed=14 * rows * width, transcendentals=rows * seq * width // HEAD_DIM
        ),
    )(lengths, qkv, do)


def pick_attn_kernel(me_ref, qkv, out, kept):
    p = pl.program_id(0)

    @pl.when(p < 3)
    def _():
        kept[...] = qkv[...]

    @pl.when(p == 3)
    def _():
        kept[...] = out[...]


def pick_attn(me, qkv_weight, out_weight, reps):
    rows, width = out_weight.shape[0], out_weight.shape[1] // reps
    return pl.pallas_call(
        pick_attn_kernel,
        grid_spec=pltpu.PrefetchScalarGridSpec(
            num_scalar_prefetch=1,
            grid=(4,),
            in_specs=[
                pl.BlockSpec((rows, width), lambda p, m: (0, jnp.minimum(p, 2) * reps + m[0])),
                pl.BlockSpec((rows, width), lambda p, m: (0, m[0])),
            ],
            out_specs=pl.BlockSpec((rows, width), lambda p, m: (0, p)),
        ),
        out_shape=jax.ShapeDtypeStruct((rows, 4 * width), BF),
        cost_estimate=pl.CostEstimate(flops=0, bytes_accessed=16 * rows * width, transcendentals=0),
    )(me.reshape(1), qkv_weight, out_weight)


def pick_ffn_kernel(me_ref, up, down, up_kept, down_kept):
    up_kept[...] = up[...]
    down_kept[...] = down[...]


def pick_ffn(me, up_weight, down_weight, reps, shards):
    rows, ff = up_weight.shape
    width = ff // (reps * shards)
    tall, dim = down_weight.shape[0] // reps, down_weight.shape[1]
    tile = dim // shards
    return pl.pallas_call(
        pick_ffn_kernel,
        grid_spec=pltpu.PrefetchScalarGridSpec(
            num_scalar_prefetch=1,
            grid=(shards,),
            in_specs=[
                pl.BlockSpec((rows, width), lambda p, m: (0, p * reps + m[0])),
                pl.BlockSpec((tall, tile), lambda p, m: (m[0], p)),
            ],
            out_specs=[
                pl.BlockSpec((rows, width), lambda p, m: (0, p)),
                pl.BlockSpec((tall, tile), lambda p, m: (0, p)),
            ],
        ),
        out_shape=[jax.ShapeDtypeStruct((rows, ff // reps), BF), jax.ShapeDtypeStruct((tall, dim), BF)],
        cost_estimate=pl.CostEstimate(flops=0, bytes_accessed=8 * rows * width * shards, transcendentals=0),
    )(me.reshape(1), up_weight, down_weight)


def place_cols_kernel(me_ref, own, ax, ay, low, high, out):
    width = own.shape[1]
    me = me_ref[0]

    def put(k, value):
        out[:, pl.ds(pl.multiple_of((me ^ k) * width, width), width)] = value.astype(out.dtype)

    put(0, own[...])
    put(1, ax[...])
    put(2, ay[...])

    @pl.when(pl.program_id(1) == 0)
    def _():
        put(3, low[...])

    @pl.when(pl.program_id(1) == 1)
    def _():
        put(3, high[...])


def place_cols(me, pieces, parts, dtype=F32):
    own, low = pieces[0], pieces[3]
    rows, cols = own.shape
    width, half = cols // parts, rows // 2
    tile = pl.BlockSpec((half, width), lambda p, t, m: (t, p))
    part = pl.BlockSpec((half, width), lambda p, t, m: (0, p))
    return pl.pallas_call(
        place_cols_kernel,
        grid_spec=pltpu.PrefetchScalarGridSpec(
            num_scalar_prefetch=1,
            grid=(parts, 2),
            in_specs=[tile, tile, tile, part, part],
            out_specs=pl.BlockSpec((half, 4 * width), lambda p, t, m: (t, p)),
        ),
        out_shape=jax.ShapeDtypeStruct((rows, 4 * cols), dtype),
        cost_estimate=pl.CostEstimate(flops=0, bytes_accessed=24 * rows * cols, transcendentals=0),
    )(me.reshape(1), *pieces)


def join_attn_kernel(me_ref, qkv, own, ax, ay, low, high, joined):
    k = pl.program_id(0)
    wide, half = qkv.shape[1], low.shape[0]
    joined[:, :wide] = qkv[...]

    @pl.when(k == 0)
    def _():
        joined[:, wide:] = own[...]

    @pl.when(k == 1)
    def _():
        joined[:, wide:] = ax[...]

    @pl.when(k == 2)
    def _():
        joined[:, wide:] = ay[...]

    @pl.when(k == 3)
    def _():
        joined[:half, wide:] = low[...]
        joined[half:, wide:] = high[...]


def join_attn(me, qkv, pieces):
    own, low = pieces[0], pieces[3]
    rows, cols = own.shape
    wide = qkv.shape[1]
    full = pl.BlockSpec((rows, cols), lambda k, m: (0, 0))
    part = pl.BlockSpec((low.shape[0], cols), lambda k, m: (0, 0))
    return pl.pallas_call(
        join_attn_kernel,
        grid_spec=pltpu.PrefetchScalarGridSpec(
            num_scalar_prefetch=1,
            grid=(4,),
            in_specs=[pl.BlockSpec((rows, wide), lambda k, m: (m[0] ^ k, 0)), full, full, full, part, part],
            out_specs=pl.BlockSpec((rows, wide + cols), lambda k, m: (m[0] ^ k, 0)),
        ),
        out_shape=jax.ShapeDtypeStruct((4 * rows, wide + cols), BF),
        cost_estimate=pl.CostEstimate(flops=0, bytes_accessed=16 * rows * (wide + cols), transcendentals=0),
    )(me.reshape(1), qkv, *pieces)


def place_attn_kernel(me_ref, own, ax, ay, low, high, qkv, out):
    width = own.shape[1]
    me = me_ref[0]
    p, t = pl.program_id(0), pl.program_id(1)

    def put(k, value):
        at = pl.ds(pl.multiple_of((me ^ k) * width, width), width)

        @pl.when(p < 3)
        def _():
            qkv[:, at] = value.astype(F32)

        @pl.when(p == 3)
        def _():
            out[:, at] = value.astype(F32)

    put(0, own[...])
    put(1, ax[...])
    put(2, ay[...])

    @pl.when(t == 0)
    def _():
        put(3, low[...])

    @pl.when(t == 1)
    def _():
        put(3, high[...])


def place_attn(me, pieces):
    own, low = pieces[0], pieces[3]
    rows, cols = own.shape
    width, half = cols // 4, rows // 2
    tile = pl.BlockSpec((half, width), lambda p, t, m: (t, p))
    part = pl.BlockSpec((half, width), lambda p, t, m: (0, p))
    return pl.pallas_call(
        place_attn_kernel,
        grid_spec=pltpu.PrefetchScalarGridSpec(
            num_scalar_prefetch=1,
            grid=(4, 2),
            in_specs=[tile, tile, tile, part, part],
            out_specs=[
                pl.BlockSpec((half, cols), lambda p, t, m: (jnp.where(p < 3, t, 1), jnp.minimum(p, 2))),
                pl.BlockSpec((half, cols), lambda p, t, m: (jnp.where(p < 3, 0, t), 0)),
            ],
        ),
        out_shape=[jax.ShapeDtypeStruct((rows, 3 * cols), F32), jax.ShapeDtypeStruct((rows, cols), F32)],
        cost_estimate=pl.CostEstimate(flops=0, bytes_accessed=24 * rows * cols, transcendentals=0),
    )(me.reshape(1), *pieces)


def place_rows_kernel(me_ref, own, ax, ay, low, high, out):
    k = pl.program_id(0)
    half = low.shape[0]

    @pl.when(k == 0)
    def _():
        out[...] = own[...].astype(out.dtype)

    @pl.when(k == 1)
    def _():
        out[...] = ax[...].astype(out.dtype)

    @pl.when(k == 2)
    def _():
        out[...] = ay[...].astype(out.dtype)

    @pl.when(k == 3)
    def _():
        out[:half] = low[...].astype(out.dtype)
        out[half:] = high[...].astype(out.dtype)


def place_rows(me, pieces, dtype=F32):
    own, low = pieces[0], pieces[3]
    rows, cols = own.shape
    full = pl.BlockSpec((rows, cols), lambda k, m: (0, 0))
    part = pl.BlockSpec((low.shape[0], cols), lambda k, m: (0, 0))
    return pl.pallas_call(
        place_rows_kernel,
        grid_spec=pltpu.PrefetchScalarGridSpec(
            num_scalar_prefetch=1,
            grid=(4,),
            in_specs=[full, full, full, part, part],
            out_specs=pl.BlockSpec((rows, cols), lambda k, m: (m[0] ^ k, 0)),
        ),
        out_shape=jax.ShapeDtypeStruct((4 * rows, cols), dtype),
        cost_estimate=pl.CostEstimate(flops=0, bytes_accessed=24 * rows * cols, transcendentals=0),
    )(me.reshape(1), *pieces)


def after(value, *deps):
    return lax.optimization_barrier((value,) + deps)[0]


def norm_forward(resid, gain, shift):
    center = resid - jnp.mean(resid, -1, keepdims=True)
    inv = lax.rsqrt(jnp.mean(center * center, -1, keepdims=True) + EPS)
    n = center * inv
    return n * gain + shift, n, inv


def norm_backward(g, gain, n, inv):
    dn = g * gain
    d = inv * (dn - jnp.mean(dn, -1, keepdims=True) - n * jnp.mean(dn * n, -1, keepdims=True))
    return d, jnp.sum(g * n, 0), jnp.sum(g, 0)


class Moves:
    def __init__(self, reps, shards):
        self.reps, self.shards = reps, shards
        self.square = reps == 4
        self.me = lax.axis_index("rep")
        self.xs = [(r, r ^ 1) for r in range(reps)]
        self.ys = [(r, r ^ 2) for r in range(reps)]
        self.ds = [(r, r ^ 3) for r in range(reps)]

    def over_x(self, a):
        return lax.ppermute(a, "rep", self.xs)

    def over_y(self, a):
        return lax.ppermute(a, "rep", self.ys)

    def gather_near(self, a):
        return a, self.over_x(a), self.over_y(a)

    def gather_far(self, near):
        own, ax, ay = near
        half = own.shape[0] // 2
        return [own, ax, ay, self.over_x(ay[:half]), self.over_y(ax[half:])]

    def gather_pieces(self, a, *meanwhile):
        near = self.gather_near(a)
        if meanwhile:
            near = lax.optimization_barrier(near + meanwhile)[:3]
        return self.gather_far(near)

    def gather_rows(self, a):
        if not self.square:
            return lax.all_gather(a, "rep", axis=0, tiled=True)
        return jnp.concatenate(self.gather_pieces(a), 0)

    def gather_small(self, a):
        if not self.square:
            return lax.all_gather(a, "rep", axis=0, tiled=True)
        return jnp.concatenate([a, self.over_x(a), self.over_y(a), lax.ppermute(a, "rep", self.ds)], 0)

    def far_term(self, left, right, product):
        rows = left.shape[0] // self.reps
        return product(left[3 * rows : 4 * rows], right).astype(BF) if self.square else None

    def scatter_sum(self, left, right, product, far, late=()):
        rows = left.shape[0] // self.reps
        block = lambda a, k: product(a[k * rows : (k + 1) * rows], right)
        if not self.square:
            whole = jnp.concatenate([block(left, k).astype(BF) for k in range(self.reps)], 0)
            return lax.psum_scatter(whole, "rep", scatter_dimension=0, tiled=True).astype(F32)
        half = rows // 2
        for_y, for_x = self.over_x(far[:half]), self.over_y(far[half:])
        left = after(left, far)
        px, py = block(left, 1), block(left, 2)
        px = jnp.concatenate([px[:half], px[half:] + for_x.astype(F32)], 0).astype(BF)
        py = jnp.concatenate([py[:half] + for_y.astype(F32), py[half:]], 0).astype(BF)
        got_x, got_y = self.over_x(px), self.over_y(py)
        return block(after(left, *late), 0) + got_x.astype(F32) + got_y.astype(F32)

    def over_both(self, a):
        return lax.ppermute(a, "rep", self.ds)

    def swap_pieces(self, take):
        got = self.over_both(take(self.me ^ 3))
        half = got.shape[0] // 2
        return [take(self.me), self.over_x(take(self.me ^ 1)), self.over_y(take(self.me ^ 2)), got[:half], got[half:]]

    def swap(self, a):
        return lax.all_to_all(a, "rep", 0, 0, tiled=True)

    def gather_weight(self, w):
        return lax.all_gather(w, "fsdp", axis=0, tiled=True)

    def own_total(self, a):
        if not self.square:
            return lax.dynamic_index_in_dim(lax.psum(a, ("rep", "fsdp")), lax.axis_index("fsdp"), 0, False)
        a = jnp.sum(lax.all_to_all(a, "fsdp", 0, 0, tiled=True), 0)
        return a + self.over_x(a) + self.over_y(a) + self.over_both(a)

    def scatter_weight(self, g):
        return lax.psum_scatter(g, "fsdp", scatter_dimension=0, tiled=True)


def per_device(
    tokens,
    lengths,
    cotangent,
    qkv_weight,
    qv_bias,
    out_weight,
    out_bias,
    attn_gain,
    attn_shift,
    up_weight,
    up_bias,
    down_weight,
    down_bias,
    ffn_gain,
    ffn_shift,
    reps,
    shards,
):
    mv = Moves(reps, shards)
    r = mv.me
    slots, seq, _ = tokens.shape
    rows = slots * seq
    ff = up_weight.shape[1]
    dr, fr = D // reps, ff // reps
    fpart = ff // (shards * reps)
    wrows = qkv_weight.shape[0]

    small = [qv_bias, out_bias, attn_gain, attn_shift, up_bias, down_bias, ffn_gain, ffn_shift]
    sizes = [s.shape[0] for s in small]
    packed = lax.all_gather(jnp.concatenate(small, 0), "fsdp", axis=0, tiled=False).astype(F32)
    full, at = [], 0
    for size in sizes:
        full.append(packed[:, at : at + size].reshape(-1))
        at += size
    b_qv, b_out, g_attn, s_attn, b_up, b_down, g_ffn, s_ffn = full
    bias_q = lax.dynamic_slice(b_qv, (r * dr,), (dr,))
    bias_v = lax.dynamic_slice(b_qv, (D + r * dr,), (dr,))
    bias_qkv = jnp.concatenate([bias_q, jnp.zeros_like(bias_q), bias_v], 0)
    bias_up = lax.dynamic_index_in_dim(b_up.reshape(shards, reps, fpart), r, 1, False).reshape(-1)

    fast = mv.square and fpart % 128 == 0
    if fast:
        attn_own = pick_attn(r, qkv_weight, out_weight, reps)
        up_own, down_own = pick_ffn(r, up_weight, down_weight, reps, shards)
        w_attn = mv.gather_weight(attn_own)
        w_qkv = w_attn[:, : 3 * dr]
        w_out = place_cols(r, mv.swap_pieces(lambda q: lax.dynamic_slice(w_attn, (q * dr, 3 * dr), (dr, dr))), 1, BF)
    else:
        pick_cols = lambda w, parts: lax.dynamic_index_in_dim(w.reshape(wrows, parts, reps, -1), r, 2, False).reshape(wrows, -1)
        up_own = pick_cols(up_weight, shards)
        down_own = lax.dynamic_slice(down_weight, (r * fpart, 0), (fpart, D))
        w_qkv = mv.gather_weight(pick_cols(qkv_weight, 3))
        w_out = mv.swap(mv.gather_weight(pick_cols(out_weight, 1)))
        w_out = w_out.reshape(reps, dr, dr).transpose(1, 0, 2).reshape(dr, D)
    w_up = mv.gather_weight(up_own)
    w_down = mv.gather_weight(down_own)

    x = tokens.reshape(rows, D)
    lens = mv.gather_small(lengths)
    x_all = mv.gather_rows(x)
    qkv = (mm(x_all, w_qkv) + bias_qkv).astype(BF)
    o = attn_fwd(lens, qkv, seq)
    attn = mv.scatter_sum(o, w_out, mm, mv.far_term(o, w_out, mm))
    x1, n1, inv1 = norm_forward(x.astype(F32) + attn + b_out, g_attn, s_attn)

    x1_all = mv.gather_rows(x1.astype(BF))
    hidden = mm(x1_all, w_up) + bias_up
    inner = 0.7978845608028654 * (hidden + 0.044715 * hidden * hidden * hidden)
    t = jnp.tanh(inner)
    act = (0.5 * hidden * (1.0 + t)).astype(BF)
    slope = 0.5 * (1.0 + t) + 0.5 * hidden * (1.0 - t * t) * (
        0.7978845608028654 * (1.0 + 3 * 0.044715 * hidden * hidden)
    )
    slope = slope.astype(BF)
    branch = mv.scatter_sum(act, w_down, mm, mv.far_term(act, w_down, mm))
    result, n2, inv2 = norm_forward(x1 + branch + b_down, g_ffn, s_ffn)
    output = result.astype(BF).reshape(slots, seq, D)

    valid = (jnp.arange(seq, dtype=jnp.int32)[None, :] < lengths[:, None]).astype(F32)
    g = cotangent.reshape(rows, D).astype(F32) * valid.reshape(rows, 1)
    dr2, d_gffn, d_sffn = norm_backward(g, g_ffn, n2, inv2)
    df = dr2.astype(BF)
    df_all = mv.gather_rows(df)
    d_wdown = mm_tn(act, df_all).astype(BF)
    df_all = after(df_all, d_wdown)
    d_wdown = mv.scatter_weight(d_wdown)
    d_bdown = jnp.sum(df.astype(F32), 0)
    dh = (mm_nt(df_all, w_down) * slope.astype(F32)).astype(BF)
    d_bup = jnp.sum(dh.astype(F32), 0)
    far = mv.far_term(dh, w_up, mm_nt)
    d_wup = mm_tn(x1_all, after(dh, far) if fast else dh).astype(BF)
    dx1 = dr2 + mv.scatter_sum(dh, w_up, mm_nt, far, (d_wup,))
    d_wup = mv.scatter_weight(d_wup)

    dr1, d_gattn, d_sattn = norm_backward(dx1, g_attn, n1, inv1)
    dt = dr1.astype(BF)
    dt_all = after(mv.gather_rows(dt), d_wdown)
    d_bout = jnp.sum(dt.astype(F32), 0)
    d_wout = mm_tn(o, dt_all).astype(BF)
    if fast:
        out_pieces = mv.swap_pieces(lambda q: lax.dynamic_slice(d_wout, (0, q * dr), (dr, dr)))
    do = mm_nt(dt_all, w_out).astype(BF)
    dqkv, sums = attn_bwd(lens, qkv, do, seq)
    d_wqkv = mm_tn(x_all, dqkv).astype(BF)
    if fast:
        down_near = mv.gather_near(after(d_wdown, dt_all))
        d_wattn = join_attn(r, after(d_wqkv, *down_near), out_pieces)
        dqkv = after(dqkv, d_wattn)
        d_wattn = mv.scatter_weight(d_wattn)
        down_pieces = mv.gather_far(down_near)
    else:
        d_wqkv = mv.scatter_weight(d_wqkv)
        d_wout = mv.swap(d_wout.reshape(dr, reps, dr).transpose(1, 0, 2).reshape(reps * dr, dr))
        d_wout = mv.scatter_weight(d_wout)

    zero = jnp.zeros((2, D), F32)
    d_qv = lax.dynamic_update_slice(zero, jnp.stack([sums[0, :dr], sums[0, 2 * dr :]]), (0, r * dr)).reshape(-1)
    d_bup = lax.dynamic_update_slice(
        jnp.zeros((shards, reps, fpart), F32), d_bup.reshape(shards, 1, fpart), (0, r, 0)
    ).reshape(-1)
    grads = [d_qv, d_bout, d_gattn, d_sattn, d_bup, d_bdown, d_gffn, d_sffn]
    packed = jnp.concatenate([v.reshape(shards, -1) for v in grads], 1)
    packed = mv.own_total(packed)

    late = (packed, d_wup, *down_pieces) if fast else ()
    input_grad = dr1 + mv.scatter_sum(dqkv, w_qkv, mm_nt, mv.far_term(dqkv, w_qkv, mm_nt), late)
    input_grad = input_grad.reshape(slots, seq, D)

    if fast:
        up_pieces = mv.gather_pieces(d_wup)
        d_wdown = place_rows(r, down_pieces)
        d_wup = place_cols(r, up_pieces, shards)
        attn_pieces = mv.gather_pieces(after(d_wattn, input_grad, *up_pieces), d_wdown, d_wup)
        d_wqkv, d_wout = place_attn(r, attn_pieces)
    else:

        def spread(shard, parts):
            whole = lax.all_gather(shard, "rep", axis=0, tiled=False).astype(F32)
            whole = whole.reshape(reps, wrows, parts, -1).transpose(1, 2, 0, 3)
            return whole.reshape(wrows, -1)

        d_wdown = mv.gather_rows(d_wdown).astype(F32)
        d_wup, d_wout, d_wqkv = spread(d_wup, shards), spread(d_wout, 1), spread(d_wqkv, 3)

    pieces, at = [], 0
    for size in sizes:
        pieces.append(packed[at : at + size])
        at += size
    d_qv, d_bout, d_gattn, d_sattn, d_bup, d_bdown, d_gffn, d_sffn = pieces
    return (
        output,
        input_grad,
        d_wqkv,
        d_qv,
        d_wout,
        d_bout,
        d_gattn,
        d_sattn,
        d_wup,
        d_bup,
        d_wdown,
        d_bdown,
        d_gffn,
        d_sffn,
    )


def solution(mesh):
    reps, shards = mesh.shape["rep"], mesh.shape["fsdp"]
    seqs = P(("rep", "fsdp"), None, None)
    mat, vec = P("fsdp", None), P("fsdp")

    def program(*args):
        return per_device(*args, reps=reps, shards=shards)

    params = (mat, vec, mat, vec, vec, vec, mat, vec, mat, vec, vec, vec)
    return jax.shard_map(
        program,
        mesh=mesh,
        in_specs=(seqs, P(("rep", "fsdp")), seqs) + params,
        out_specs=(seqs, seqs) + params,
        check_vma=False,
    )
```

```python
import jax
import jax.numpy as jnp
from jax import lax
from jax.experimental import pallas as pl
from jax.experimental.pallas import tpu as pltpu
from jax.sharding import PartitionSpec as P

D = 2048
HEADS = 16
HEAD_DIM = 128
EPS = 1e-05
PAD = 16
BF = jnp.bfloat16
F32 = jnp.float32


def mm(a, b):
    return jnp.dot(a, b, preferred_element_type=F32)


def mm_nt(a, b):
    return lax.dot_general(a, b, (((1,), (1,)), ((), ())), preferred_element_type=F32)


def mm_tn(a, b):
    return lax.dot_general(a, b, (((0,), (0,)), ((), ())), preferred_element_type=F32)


SLOTS = 2


def heads_of(qkv_ref, width, seq):
    return [
        (slot, slice(slot * seq, (slot + 1) * seq), [part * width + at for part in range(3)])
        for slot in range(SLOTS)
        for at in range(0, width, HEAD_DIM)
    ]


def cut(ref, rows, at):
    return ref[rows, at : at + HEAD_DIM]


def all_probs(len_ref, qkv_ref, heads):
    scores = [mm_nt(cut(qkv_ref, rows, at[0]), cut(qkv_ref, rows, at[1])) * HEAD_DIM**-0.5 for _, rows, at in heads]
    cols = lax.broadcasted_iota(jnp.int32, scores[0].shape, 1)
    first = pl.program_id(0) * SLOTS
    valid = [cols < len_ref[first + slot] for slot in range(SLOTS)]
    scores = [jnp.where(valid[slot], s, -1000000000.0) for s, (slot, _, _) in zip(scores, heads)]
    expo = [jnp.exp(s - jnp.max(s, -1, keepdims=True)) for s in scores]
    return [e / jnp.sum(e, -1, keepdims=True) for e in expo]


def attn_fwd_kernel(len_ref, qkv_ref, o_ref, seq):
    heads = heads_of(qkv_ref, o_ref.shape[1], seq)
    probs = all_probs(len_ref, qkv_ref, heads)
    for p, (_, rows, at) in zip(probs, heads):
        o_ref[rows, at[0] : at[0] + HEAD_DIM] = mm(p.astype(BF), cut(qkv_ref, rows, at[2])).astype(BF)


def attn_bwd_kernel(len_ref, qkv_ref, do_ref, dqkv_ref, sums_ref, seq):
    width = do_ref.shape[1]
    factor = HEAD_DIM**-0.5
    heads = heads_of(qkv_ref, width, seq)
    dps = [mm_nt(cut(do_ref, rows, at[0]), cut(qkv_ref, rows, at[2])) for _, rows, at in heads]
    probs = all_probs(len_ref, qkv_ref, heads)
    lows = [p.astype(BF) for p in probs]
    dss = [(p * (dp - jnp.sum(p * dp, -1, keepdims=True))).astype(BF) for p, dp in zip(probs, dps)]
    totals = {}
    for p, ds, (_, rows, at) in zip(lows, dss, heads):
        grads = (
            (mm(ds, cut(qkv_ref, rows, at[1])) * factor).astype(BF),
            (mm_tn(ds, cut(qkv_ref, rows, at[0])) * factor).astype(BF),
            mm_tn(p, cut(do_ref, rows, at[0])).astype(BF),
        )
        for part, grad in enumerate(grads):
            dqkv_ref[rows, at[part] : at[part] + HEAD_DIM] = grad
            if part != 1:
                total = jnp.sum(grad.astype(F32), 0, keepdims=True)
                totals[at[part]] = totals[at[part]] + total if at[part] in totals else total

    @pl.when(pl.program_id(0) == 0)
    def _():
        sums_ref[...] = jnp.zeros_like(sums_ref)

    for start, total in totals.items():
        sums_ref[:, start : start + HEAD_DIM] += total


def attn_fwd(lengths, qkv, seq):
    rows, wide = qkv.shape
    width = wide // 3
    return pl.pallas_call(
        lambda *refs: attn_fwd_kernel(*refs, seq=seq),
        grid_spec=pltpu.PrefetchScalarGridSpec(
            num_scalar_prefetch=1,
            grid=(rows // (SLOTS * seq),),
            in_specs=[pl.BlockSpec((SLOTS * seq, wide), lambda i, n: (i, 0))],
            out_specs=pl.BlockSpec((SLOTS * seq, width), lambda i, n: (i, 0)),
        ),
        out_shape=jax.ShapeDtypeStruct((rows, width), BF),
        cost_estimate=pl.CostEstimate(
            flops=4 * rows * seq * width, bytes_accessed=8 * rows * width, transcendentals=rows * seq * width // HEAD_DIM
        ),
    )(lengths, qkv)


def attn_bwd(lengths, qkv, do, seq):
    rows, wide = qkv.shape
    width = wide // 3
    return pl.pallas_call(
        lambda *refs: attn_bwd_kernel(*refs, seq=seq),
        grid_spec=pltpu.PrefetchScalarGridSpec(
            num_scalar_prefetch=1,
            grid=(rows // (SLOTS * seq),),
            in_specs=[
                pl.BlockSpec((SLOTS * seq, wide), lambda i, n: (i, 0)),
                pl.BlockSpec((SLOTS * seq, width), lambda i, n: (i, 0)),
            ],
            out_specs=[
                pl.BlockSpec((SLOTS * seq, wide), lambda i, n: (i, 0)),
                pl.BlockSpec((1, wide), lambda i, n: (0, 0)),
            ],
        ),
        out_shape=[jax.ShapeDtypeStruct((rows, wide), BF), jax.ShapeDtypeStruct((1, wide), F32)],
        cost_estimate=pl.CostEstimate(
            flops=10 * rows * seq * width, bytes_accessed=14 * rows * width, transcendentals=rows * seq * width // HEAD_DIM
        ),
    )(lengths, qkv, do)


def hidden_grad_kernel(df_ref, w_ref, slope_ref, dh_ref, sums_ref):
    dh = (mm_nt(df_ref[...], w_ref[...]) * slope_ref[...].astype(F32)).astype(BF)
    dh_ref[...] = dh
    sums_ref[...] = jnp.sum(dh.astype(F32), 0, keepdims=True)


def hidden_grad(df, w_down, slope):
    rows, dim = df.shape
    units = w_down.shape[0]
    tile = 256
    return pl.pallas_call(
        hidden_grad_kernel,
        grid=(units // tile,),
        in_specs=[
            pl.BlockSpec((rows, dim), lambda i: (0, 0)),
            pl.BlockSpec((tile, dim), lambda i: (i, 0)),
            pl.BlockSpec((rows, tile), lambda i: (0, i)),
        ],
        out_specs=[pl.BlockSpec((rows, tile), lambda i: (0, i)), pl.BlockSpec((1, tile), lambda i: (0, i))],
        out_shape=[jax.ShapeDtypeStruct((rows, units), BF), jax.ShapeDtypeStruct((1, units), F32)],
        compiler_params=pltpu.CompilerParams(vmem_limit_bytes=56 * 2**20),
        cost_estimate=pl.CostEstimate(
            flops=2 * rows * dim * units, bytes_accessed=2 * (rows * dim + units * dim + 2 * rows * units), transcendentals=0
        ),
    )(df, w_down, slope)


def pick_attn_kernel(me_ref, qkv, out, kept):
    p = pl.program_id(0)

    @pl.when(p < 3)
    def _():
        kept[...] = qkv[...]

    @pl.when(p == 3)
    def _():
        kept[...] = out[...]


def pick_attn(me, qkv_weight, out_weight, reps):
    rows, width = out_weight.shape[0], out_weight.shape[1] // reps
    return pl.pallas_call(
        pick_attn_kernel,
        grid_spec=pltpu.PrefetchScalarGridSpec(
            num_scalar_prefetch=1,
            grid=(4,),
            in_specs=[
                pl.BlockSpec((rows, width), lambda p, m: (0, jnp.minimum(p, 2) * reps + m[0])),
                pl.BlockSpec((rows, width), lambda p, m: (0, m[0])),
            ],
            out_specs=pl.BlockSpec((rows, width), lambda p, m: (0, p)),
        ),
        out_shape=jax.ShapeDtypeStruct((rows, 4 * width), BF),
        cost_estimate=pl.CostEstimate(flops=0, bytes_accessed=16 * rows * width, transcendentals=0),
    )(me.reshape(1), qkv_weight, out_weight)


def pick_ffn_kernel(me_ref, up, down, up_kept, down_kept):
    up_kept[...] = up[...]
    down_kept[...] = down[...]


def pick_ffn(me, up_weight, down_weight, reps, shards):
    rows, ff = up_weight.shape
    width = ff // (reps * shards)
    tall, dim = down_weight.shape[0] // reps, down_weight.shape[1]
    tile = dim // shards
    return pl.pallas_call(
        pick_ffn_kernel,
        grid_spec=pltpu.PrefetchScalarGridSpec(
            num_scalar_prefetch=1,
            grid=(shards,),
            in_specs=[
                pl.BlockSpec((rows, width), lambda p, m: (0, p * reps + m[0])),
                pl.BlockSpec((tall, tile), lambda p, m: (m[0], p)),
            ],
            out_specs=[
                pl.BlockSpec((rows, width), lambda p, m: (0, p)),
                pl.BlockSpec((tall, tile), lambda p, m: (0, p)),
            ],
        ),
        out_shape=[jax.ShapeDtypeStruct((rows, ff // reps), BF), jax.ShapeDtypeStruct((tall, dim), BF)],
        cost_estimate=pl.CostEstimate(flops=0, bytes_accessed=8 * rows * width * shards, transcendentals=0),
    )(me.reshape(1), up_weight, down_weight)


def place_cols_kernel(me_ref, own, ax, ay, low, high, out, parts):
    width = own.shape[1] // parts
    me = me_ref[0]
    t, tiles = pl.program_id(0), pl.num_programs(0)

    def put(k, piece):
        for p in range(parts):
            at = pl.multiple_of((p * 4 + (me ^ k)) * width, width)
            out[:, pl.ds(at, width)] = piece[:, p * width : (p + 1) * width].astype(out.dtype)

    put(0, own)
    put(1, ax)
    put(2, ay)

    @pl.when(t < tiles // 2)
    def _():
        put(3, low)

    @pl.when(t >= tiles // 2)
    def _():
        put(3, high)


def place_cols(me, pieces, parts, dtype=F32):
    cols = pieces[0].shape[1]
    rows = 2 * pieces[3].shape[0]
    tile = 64 if parts > 1 else 128
    half = rows // (2 * tile)
    full = pl.BlockSpec((tile, cols), lambda t, m: (t, 0))
    return pl.pallas_call(
        lambda *refs: place_cols_kernel(*refs, parts=parts),
        grid_spec=pltpu.PrefetchScalarGridSpec(
            num_scalar_prefetch=1,
            grid=(rows // tile,),
            in_specs=[
                full,
                full,
                full,
                pl.BlockSpec((tile, cols), lambda t, m: (jnp.minimum(t, half - 1), 0)),
                pl.BlockSpec((tile, cols), lambda t, m: (jnp.maximum(t - half, 0), 0)),
            ],
            out_specs=pl.BlockSpec((tile, 4 * cols), lambda t, m: (t, 0)),
        ),
        out_shape=jax.ShapeDtypeStruct((rows, 4 * cols), dtype),
        cost_estimate=pl.CostEstimate(flops=0, bytes_accessed=24 * rows * cols, transcendentals=0),
    )(me.reshape(1), *pieces)


def out_grad_kernel(me_ref, own, ax, ay, low, high, dt, small, joined):
    k = pl.program_id(0)
    per, tall, _ = joined.shape
    kept, rows, half = tall - PAD, dt.shape[0] // 4, low.shape[0]
    joined[:, kept:, :] = small[...]

    def heads(of, block):
        if of < 3:
            return (own, ax, ay)[of][block * rows : (block + 1) * rows, :]
        ref, at = (low, block * rows) if block * rows < half else (high, block * rows - half)
        return ref[at : at + rows, :]

    def put(of):
        grad = sum(mm_tn(heads(of, n ^ of), dt[n * rows : (n + 1) * rows, :]) for n in range(4)).astype(BF)
        for i in range(per):
            joined[i, :kept, :] = grad[i * kept : (i + 1) * kept, :]

    for of in range(4):
        pl.when(k == of)(lambda of=of: put(of))


def out_grad(me, pieces, dt, small):
    own, low = pieces[0], pieces[3]
    rows, cols = own.shape
    shards = small.shape[0]
    per = shards // 4
    tall = cols // per + PAD
    full = pl.BlockSpec((rows, cols), lambda k, m: (0, 0))
    part = pl.BlockSpec((low.shape[0], cols), lambda k, m: (0, 0))
    return pl.pallas_call(
        out_grad_kernel,
        grid_spec=pltpu.PrefetchScalarGridSpec(
            num_scalar_prefetch=1,
            grid=(4,),
            in_specs=[full, full, full, part, part]
            + [
                pl.BlockSpec((rows, cols), lambda k, m: (0, m[0])),
                pl.BlockSpec((per, PAD, cols), lambda k, m: (m[0] ^ k, 0, 0)),
            ],
            out_specs=pl.BlockSpec((per, tall, cols), lambda k, m: (m[0] ^ k, 0, 0)),
        ),
        out_shape=jax.ShapeDtypeStruct((shards, tall, cols), BF),
        compiler_params=pltpu.CompilerParams(vmem_limit_bytes=40 * 2**20),
        cost_estimate=pl.CostEstimate(flops=8 * rows * cols * cols, bytes_accessed=14 * rows * cols, transcendentals=0),
    )(me.reshape(1), *pieces, dt, small)


def place_rows_kernel(me_ref, own, ax, ay, low, high, out):
    k = pl.program_id(0)
    half = low.shape[0]

    @pl.when(k == 0)
    def _():
        out[...] = own[...].astype(out.dtype)

    @pl.when(k == 1)
    def _():
        out[...] = ax[...].astype(out.dtype)

    @pl.when(k == 2)
    def _():
        out[...] = ay[...].astype(out.dtype)

    @pl.when(k == 3)
    def _():
        out[:half] = low[...].astype(out.dtype)
        out[half:] = high[...].astype(out.dtype)


def place_rows(me, pieces, dtype=F32):
    own, low = pieces[0], pieces[3]
    rows, cols = own.shape
    full = pl.BlockSpec((rows, cols), lambda k, m: (0, 0))
    part = pl.BlockSpec((low.shape[0], cols), lambda k, m: (0, 0))
    return pl.pallas_call(
        place_rows_kernel,
        grid_spec=pltpu.PrefetchScalarGridSpec(
            num_scalar_prefetch=1,
            grid=(4,),
            in_specs=[full, full, full, part, part],
            out_specs=pl.BlockSpec((rows, cols), lambda k, m: (m[0] ^ k, 0)),
        ),
        out_shape=jax.ShapeDtypeStruct((4 * rows, cols), dtype),
        cost_estimate=pl.CostEstimate(flops=0, bytes_accessed=24 * rows * cols, transcendentals=0),
    )(me.reshape(1), *pieces)


def after(value, *deps):
    return lax.optimization_barrier((value,) + deps)[0]


def norm_forward(resid, gain, shift):
    center = resid - jnp.mean(resid, -1, keepdims=True)
    inv = lax.rsqrt(jnp.mean(center * center, -1, keepdims=True) + EPS)
    n = center * inv
    return n * gain + shift, n, inv


def norm_backward(g, gain, n, inv):
    dn = g * gain
    d = inv * (dn - jnp.mean(dn, -1, keepdims=True) - n * jnp.mean(dn * n, -1, keepdims=True))
    return d, jnp.sum(g * n, 0), jnp.sum(g, 0)


class Moves:
    def __init__(self, reps, shards):
        self.reps, self.shards = reps, shards
        self.square = reps == 4
        self.me = lax.axis_index("rep")
        self.xs = [(r, r ^ 1) for r in range(reps)]
        self.ys = [(r, r ^ 2) for r in range(reps)]
        self.ds = [(r, r ^ 3) for r in range(reps)]

    def over_x(self, a):
        return lax.ppermute(a, "rep", self.xs)

    def over_y(self, a):
        return lax.ppermute(a, "rep", self.ys)

    def gather_near(self, a):
        return a, self.over_x(a), self.over_y(a)

    def gather_far(self, near):
        own, ax, ay = near
        half = own.shape[0] // 32 * 16
        return [own, ax, ay, self.over_x(ay[:half]), self.over_y(ax[half:])]

    def gather_pieces(self, a, *meanwhile):
        near = self.gather_near(a)
        if meanwhile:
            near = lax.optimization_barrier(near + meanwhile)[:3]
        return self.gather_far(near)

    def gather_direct(self, a):
        half = a.shape[0] // 32 * 16
        both = self.over_both(a)
        return [a, self.over_x(a), self.over_y(a), both[:half], both[half:]]

    def gather_rows(self, a):
        if not self.square:
            return lax.all_gather(a, "rep", axis=0, tiled=True)
        return jnp.concatenate(self.gather_pieces(a), 0)

    def gather_small(self, a):
        if not self.square:
            return lax.all_gather(a, "rep", axis=0, tiled=True)
        return jnp.concatenate([a, self.over_x(a), self.over_y(a), lax.ppermute(a, "rep", self.ds)], 0)

    def scatter_sum(self, left, right, product, whole=False, between=None, first=()):
        rows = left.shape[0] // self.reps
        full = product(left, right) if whole or not self.square else None
        if not self.square:
            return lax.psum_scatter(full.astype(BF), "rep", scatter_dimension=0, tiled=True).astype(F32)
        cut = lambda a, k: a[k * rows : (k + 1) * rows]
        block = lambda a, k: cut(full, k) if whole else product(cut(a, k), right)
        half = rows // 2
        if whole:
            full = after(full, *first)
        far = block(left, 3).astype(BF)
        for_y, for_x = self.over_x(far[:half]), self.over_y(far[half:])
        left = after(left, far)
        px, py = block(left, 1), block(left, 2)
        px = jnp.concatenate([px[:half], px[half:] + for_x.astype(F32)], 0).astype(BF)
        py = jnp.concatenate([py[:half] + for_y.astype(F32), py[half:]], 0).astype(BF)
        got_x, got_y = self.over_x(px), self.over_y(py)
        own = block(left, 0)
        if between is not None:
            own = after(own, *between(px, py))
        return own + got_x.astype(F32) + got_y.astype(F32)

    def over_both(self, a):
        return lax.ppermute(a, "rep", self.ds)

    def swap_pieces(self, take):
        got = self.over_both(take(self.me ^ 3))
        half = got.shape[0] // 2
        return [take(self.me), self.over_x(take(self.me ^ 1)), self.over_y(take(self.me ^ 2)), got[:half], got[half:]]

    def swap(self, a):
        return lax.all_to_all(a, "rep", 0, 0, tiled=True)

    def gather_weight(self, w):
        return lax.all_gather(w, "fsdp", axis=0, tiled=True)

    def own_total(self, a):
        return lax.dynamic_index_in_dim(lax.psum(a, ("rep", "fsdp")), lax.axis_index("fsdp"), 0, False)

    def scatter_weight(self, g):
        return lax.psum_scatter(g, "fsdp", scatter_dimension=0, tiled=True)


def per_device(
    tokens,
    lengths,
    cotangent,
    qkv_weight,
    qv_bias,
    out_weight,
    out_bias,
    attn_gain,
    attn_shift,
    up_weight,
    up_bias,
    down_weight,
    down_bias,
    ffn_gain,
    ffn_shift,
    reps,
    shards,
):
    mv = Moves(reps, shards)
    r = mv.me
    slots, seq, _ = tokens.shape
    rows = slots * seq
    ff = up_weight.shape[1]
    dr, fr = D // reps, ff // reps
    fpart = ff // (shards * reps)
    wrows = qkv_weight.shape[0]

    small = [qv_bias, out_bias, attn_gain, attn_shift, up_bias, down_bias, ffn_gain, ffn_shift]
    sizes = [s.shape[0] for s in small]
    packed = lax.all_gather(jnp.concatenate(small, 0), "fsdp", axis=0, tiled=False).astype(F32)
    full, at = [], 0
    for size in sizes:
        full.append(packed[:, at : at + size].reshape(-1))
        at += size
    b_qv, b_out, g_attn, s_attn, b_up, b_down, g_ffn, s_ffn = full
    bias_q = lax.dynamic_slice(b_qv, (r * dr,), (dr,))
    bias_v = lax.dynamic_slice(b_qv, (D + r * dr,), (dr,))
    bias_qkv = jnp.concatenate([bias_q, jnp.zeros_like(bias_q), bias_v], 0)
    bias_up = lax.dynamic_index_in_dim(b_up.reshape(shards, reps, fpart), r, 1, False).reshape(-1)

    fast = mv.square and fpart % 128 == 0
    if fast:
        attn_own = pick_attn(r, qkv_weight, out_weight, reps)
        up_own, down_own = pick_ffn(r, up_weight, down_weight, reps, shards)
        w_attn = mv.gather_weight(attn_own)
        w_qkv = w_attn[:, : 3 * dr]
        w_out = place_cols(r, mv.swap_pieces(lambda q: lax.dynamic_slice(w_attn, (q * dr, 3 * dr), (dr, dr))), 1, BF)
    else:
        pick_cols = lambda w, parts: lax.dynamic_index_in_dim(w.reshape(wrows, parts, reps, -1), r, 2, False).reshape(wrows, -1)
        up_own = pick_cols(up_weight, shards)
        down_own = lax.dynamic_slice(down_weight, (r * fpart, 0), (fpart, D))
        w_qkv = mv.gather_weight(pick_cols(qkv_weight, 3))
        w_out = mv.swap(mv.gather_weight(pick_cols(out_weight, 1)))
        w_out = w_out.reshape(reps, dr, dr).transpose(1, 0, 2).reshape(dr, D)
    w_up = mv.gather_weight(up_own)
    w_down = mv.gather_weight(down_own)

    x = tokens.reshape(rows, D)
    lens = mv.gather_small(lengths)
    x_all = mv.gather_rows(x)
    qkv = (mm(x_all, w_qkv) + bias_qkv).astype(BF)
    o = attn_fwd(lens, qkv, seq)
    attn = mv.scatter_sum(o, w_out, mm)
    x1, n1, inv1 = norm_forward(x.astype(F32) + attn + b_out, g_attn, s_attn)

    x1_all = mv.gather_rows(x1.astype(BF))
    hidden = mm(x1_all, w_up) + bias_up
    inner = 0.7978845608028654 * (hidden + 0.044715 * hidden * hidden * hidden)
    t = jnp.tanh(inner)
    act = (0.5 * hidden * (1.0 + t)).astype(BF)
    slope = 0.5 * (1.0 + t) + 0.5 * hidden * (1.0 - t * t) * (
        0.7978845608028654 * (1.0 + 3 * 0.044715 * hidden * hidden)
    )
    slope = slope.astype(BF)
    if fast:
        o_pieces = mv.gather_pieces(after(o, x1_all))
        act = after(act, *o_pieces)
    branch = mv.scatter_sum(act, w_down, mm)
    result, n2, inv2 = norm_forward(x1 + branch + b_down, g_ffn, s_ffn)
    output = result.astype(BF).reshape(slots, seq, D)

    valid = (jnp.arange(seq, dtype=jnp.int32)[None, :] < lengths[:, None]).astype(F32)
    g = cotangent.reshape(rows, D).astype(F32) * valid.reshape(rows, 1)
    dr2, d_gffn, d_sffn = norm_backward(g, g_ffn, n2, inv2)
    df = dr2.astype(BF)
    df_all = mv.gather_rows(df)
    d_wdown = mm_tn(act, df_all).astype(BF)
    df_all = after(df_all, d_wdown)
    d_wdown = mv.scatter_weight(d_wdown)
    d_bdown = jnp.sum(df.astype(F32), 0)
    dh, d_bup = hidden_grad(df_all, w_down, slope)
    def up_grad(*sent):
        return [mm_tn(x1_all, after(dh, *sent)).astype(BF)]

    kept = []

    def keep_up_grad(*sent):
        kept.extend(up_grad(*sent))
        return kept

    dx1 = dr2 + mv.scatter_sum(dh, w_up, mm_nt, True, keep_up_grad)
    d_wup = mv.scatter_weight((kept or up_grad())[0])

    dr1, d_gattn, d_sattn = norm_backward(dx1, g_attn, n1, inv1)
    dt = dr1.astype(BF)
    dt_all = after(mv.gather_rows(dt), d_wdown)
    d_bout = jnp.sum(dt.astype(F32), 0)
    do = mm_nt(dt_all, w_out).astype(BF)
    dqkv, sums = attn_bwd(lens, qkv, do, seq)
    if fast:
        down_near = mv.gather_near(after(d_wdown, dt_all))
        x_all = after(x_all, *down_near)
    d_wqkv = mm_tn(x_all, dqkv).astype(BF)
    if fast:
        dqkv = after(dqkv, d_wqkv)
        down_pieces = mv.gather_far(down_near)
    d_wqkv = mv.scatter_weight(d_wqkv)

    zero = jnp.zeros((2, D), F32)
    d_qv = lax.dynamic_update_slice(zero, jnp.stack([sums[0, :dr], sums[0, 2 * dr :]]), (0, r * dr)).reshape(-1)
    d_bup = lax.dynamic_update_slice(
        jnp.zeros((shards, reps, fpart), F32), d_bup.reshape(shards, 1, fpart), (0, r, 0)
    ).reshape(-1)
    grads = [d_qv, d_bout, d_gattn, d_sattn, d_bup, d_bdown, d_gffn, d_sffn]
    packed = jnp.concatenate([v.reshape(shards, -1) for v in grads], 1)
    if fast:
        small = packed.astype(BF).reshape(shards, -1, dr)
        small = jnp.pad(small, ((0, 0), (0, PAD - small.shape[1]), (0, 0)))
    else:
        packed = mv.own_total(packed)

    def late_grads(*sent):
        if fast:
            up_near = mv.gather_near(after(d_wup, *sent))
            placed = place_rows(r, after(down_pieces, *up_near))
            d_wout = out_grad(r, o_pieces, after(dt_all, *sent), small)
            kept.extend([d_wout.reshape(-1, dr), placed, up_near])
            return kept[:1]
        grad = mm_tn(after(o, *sent), dt_all).astype(BF)
        return [mv.swap(grad.reshape(dr, reps, dr).transpose(1, 0, 2).reshape(reps * dr, dr))]

    kept = []
    input_grad = dr1 + mv.scatter_sum(dqkv, w_qkv, mm_nt, True, late_grads, down_pieces if fast else ())
    d_wout = mv.scatter_weight((kept or late_grads())[0])
    input_grad = input_grad.reshape(slots, seq, D)

    if fast:
        d_wdown = kept[1]
        up_pieces = mv.gather_far(kept[2])
        d_wup = place_cols(r, up_pieces, shards)
        qkv_near = mv.gather_near(after(d_wqkv, *up_pieces))
        qkv_pieces = mv.gather_far(after(qkv_near, d_wup))
        d_wqkv = place_cols(r, qkv_pieces, 3)
        out_pieces = mv.gather_direct(after(d_wout, input_grad, d_wdown, d_wqkv))
        d_wout = place_cols(r, out_pieces, 1)
        below = [p[wrows:] for p in out_pieces[:3]] + [out_pieces[4][wrows - out_pieces[3].shape[0] :]]
        packed = sum(p.astype(F32) for p in below).reshape(-1)[: sum(sizes)]
    else:

        def spread(shard, parts):
            whole = lax.all_gather(shard, "rep", axis=0, tiled=False).astype(F32)
            whole = whole.reshape(reps, wrows, parts, -1).transpose(1, 2, 0, 3)
            return whole.reshape(wrows, -1)

        d_wdown = mv.gather_rows(d_wdown).astype(F32)
        d_wup, d_wout, d_wqkv = spread(d_wup, shards), spread(d_wout, 1), spread(d_wqkv, 3)

    pieces, at = [], 0
    for size in sizes:
        pieces.append(packed[at : at + size])
        at += size
    d_qv, d_bout, d_gattn, d_sattn, d_bup, d_bdown, d_gffn, d_sffn = pieces
    return (
        output,
        input_grad,
        d_wqkv,
        d_qv,
        d_wout,
        d_bout,
        d_gattn,
        d_sattn,
        d_wup,
        d_bup,
        d_wdown,
        d_bdown,
        d_gffn,
        d_sffn,
    )


def solution(mesh):
    reps, shards = mesh.shape["rep"], mesh.shape["fsdp"]
    seqs = P(("rep", "fsdp"), None, None)
    mat, vec = P("fsdp", None), P("fsdp")

    def program(*args):
        return per_device(*args, reps=reps, shards=shards)

    params = (mat, vec, mat, vec, vec, vec, mat, vec, mat, vec, vec, vec)
    return jax.shard_map(
        program,
        mesh=mesh,
        in_specs=(seqs, P(("rep", "fsdp")), seqs) + params,
        out_specs=(seqs, seqs) + params,
        check_vma=False,
    )
```

```python
import jax
import jax.numpy as jnp
from jax import lax
from jax.experimental import pallas as pl
from jax.experimental.pallas import tpu as pltpu
from jax.sharding import PartitionSpec as P

D = 2048
HEADS = 16
HEAD_DIM = 128
EPS = 1e-05
PAD = 16
BF = jnp.bfloat16
F32 = jnp.float32


def mm(a, b):
    return jnp.dot(a, b, preferred_element_type=F32)


def mm_nt(a, b):
    return lax.dot_general(a, b, (((1,), (1,)), ((), ())), preferred_element_type=F32)


def mm_tn(a, b):
    return lax.dot_general(a, b, (((0,), (0,)), ((), ())), preferred_element_type=F32)


SLOTS = 2


def heads_of(qkv_ref, width, seq):
    return [
        (slot, slice(slot * seq, (slot + 1) * seq), [part * width + at for part in range(3)])
        for slot in range(SLOTS)
        for at in range(0, width, HEAD_DIM)
    ]


def cut(ref, rows, at):
    return ref[rows, at : at + HEAD_DIM]


def all_probs(len_ref, qkv_ref, heads):
    scores = [mm_nt(cut(qkv_ref, rows, at[0]), cut(qkv_ref, rows, at[1])) * HEAD_DIM**-0.5 for _, rows, at in heads]
    cols = lax.broadcasted_iota(jnp.int32, scores[0].shape, 1)
    first = pl.program_id(0) * SLOTS
    valid = [cols < len_ref[first + slot] for slot in range(SLOTS)]
    scores = [jnp.where(valid[slot], s, -1000000000.0) for s, (slot, _, _) in zip(scores, heads)]
    expo = [jnp.exp(s - jnp.max(s, -1, keepdims=True)) for s in scores]
    return [e / jnp.sum(e, -1, keepdims=True) for e in expo]


def attn_fwd_kernel(len_ref, qkv_ref, o_ref, seq):
    heads = heads_of(qkv_ref, o_ref.shape[1], seq)
    probs = all_probs(len_ref, qkv_ref, heads)
    for p, (_, rows, at) in zip(probs, heads):
        o_ref[rows, at[0] : at[0] + HEAD_DIM] = mm(p.astype(BF), cut(qkv_ref, rows, at[2])).astype(BF)


def attn_bwd_kernel(len_ref, qkv_ref, do_ref, dqkv_ref, sums_ref, seq):
    width = do_ref.shape[1]
    factor = HEAD_DIM**-0.5
    heads = heads_of(qkv_ref, width, seq)
    dps = [mm_nt(cut(do_ref, rows, at[0]), cut(qkv_ref, rows, at[2])) for _, rows, at in heads]
    probs = all_probs(len_ref, qkv_ref, heads)
    lows = [p.astype(BF) for p in probs]
    dss = [(p * (dp - jnp.sum(p * dp, -1, keepdims=True))).astype(BF) for p, dp in zip(probs, dps)]
    totals = {}
    for p, ds, (_, rows, at) in zip(lows, dss, heads):
        grads = (
            (mm(ds, cut(qkv_ref, rows, at[1])) * factor).astype(BF),
            (mm_tn(ds, cut(qkv_ref, rows, at[0])) * factor).astype(BF),
            mm_tn(p, cut(do_ref, rows, at[0])).astype(BF),
        )
        for part, grad in enumerate(grads):
            dqkv_ref[rows, at[part] : at[part] + HEAD_DIM] = grad
            if part != 1:
                total = jnp.sum(grad.astype(F32), 0, keepdims=True)
                totals[at[part]] = totals[at[part]] + total if at[part] in totals else total

    @pl.when(pl.program_id(0) == 0)
    def _():
        sums_ref[...] = jnp.zeros_like(sums_ref)

    for start, total in totals.items():
        sums_ref[:, start : start + HEAD_DIM] += total


def attn_fwd(lengths, qkv, seq):
    rows, wide = qkv.shape
    width = wide // 3
    return pl.pallas_call(
        lambda *refs: attn_fwd_kernel(*refs, seq=seq),
        grid_spec=pltpu.PrefetchScalarGridSpec(
            num_scalar_prefetch=1,
            grid=(rows // (SLOTS * seq),),
            in_specs=[pl.BlockSpec((SLOTS * seq, wide), lambda i, n: (i, 0))],
            out_specs=pl.BlockSpec((SLOTS * seq, width), lambda i, n: (i, 0)),
        ),
        out_shape=jax.ShapeDtypeStruct((rows, width), BF),
        cost_estimate=pl.CostEstimate(
            flops=4 * rows * seq * width, bytes_accessed=8 * rows * width, transcendentals=rows * seq * width // HEAD_DIM
        ),
    )(lengths, qkv)


def attn_bwd(lengths, qkv, do, seq):
    rows, wide = qkv.shape
    width = wide // 3
    return pl.pallas_call(
        lambda *refs: attn_bwd_kernel(*refs, seq=seq),
        grid_spec=pltpu.PrefetchScalarGridSpec(
            num_scalar_prefetch=1,
            grid=(rows // (SLOTS * seq),),
            in_specs=[
                pl.BlockSpec((SLOTS * seq, wide), lambda i, n: (i, 0)),
                pl.BlockSpec((SLOTS * seq, width), lambda i, n: (i, 0)),
            ],
            out_specs=[
                pl.BlockSpec((SLOTS * seq, wide), lambda i, n: (i, 0)),
                pl.BlockSpec((1, wide), lambda i, n: (0, 0)),
            ],
        ),
        out_shape=[jax.ShapeDtypeStruct((rows, wide), BF), jax.ShapeDtypeStruct((1, wide), F32)],
        cost_estimate=pl.CostEstimate(
            flops=10 * rows * seq * width, bytes_accessed=14 * rows * width, transcendentals=rows * seq * width // HEAD_DIM
        ),
    )(lengths, qkv, do)


def hidden_grad_kernel(df_ref, w_ref, slope_ref, dh_ref, sums_ref):
    dh = (mm_nt(df_ref[...], w_ref[...]) * slope_ref[...].astype(F32)).astype(BF)
    dh_ref[...] = dh
    sums_ref[...] = jnp.sum(dh.astype(F32), 0, keepdims=True)


def hidden_grad(df, w_down, slope):
    rows, dim = df.shape
    units = w_down.shape[0]
    tile = 256
    return pl.pallas_call(
        hidden_grad_kernel,
        grid=(units // tile,),
        in_specs=[
            pl.BlockSpec((rows, dim), lambda i: (0, 0)),
            pl.BlockSpec((tile, dim), lambda i: (i, 0)),
            pl.BlockSpec((rows, tile), lambda i: (0, i)),
        ],
        out_specs=[pl.BlockSpec((rows, tile), lambda i: (0, i)), pl.BlockSpec((1, tile), lambda i: (0, i))],
        out_shape=[jax.ShapeDtypeStruct((rows, units), BF), jax.ShapeDtypeStruct((1, units), F32)],
        compiler_params=pltpu.CompilerParams(vmem_limit_bytes=56 * 2**20),
        cost_estimate=pl.CostEstimate(
            flops=2 * rows * dim * units, bytes_accessed=2 * (rows * dim + units * dim + 2 * rows * units), transcendentals=0
        ),
    )(df, w_down, slope)


def pick_attn_kernel(me_ref, qkv, out, kept):
    p = pl.program_id(0)

    @pl.when(p < 3)
    def _():
        kept[...] = qkv[...]

    @pl.when(p == 3)
    def _():
        kept[...] = out[...]


def pick_attn(me, qkv_weight, out_weight, reps):
    rows, width = out_weight.shape[0], out_weight.shape[1] // reps
    return pl.pallas_call(
        pick_attn_kernel,
        grid_spec=pltpu.PrefetchScalarGridSpec(
            num_scalar_prefetch=1,
            grid=(4,),
            in_specs=[
                pl.BlockSpec((rows, width), lambda p, m: (0, jnp.minimum(p, 2) * reps + m[0])),
                pl.BlockSpec((rows, width), lambda p, m: (0, m[0])),
            ],
            out_specs=pl.BlockSpec((rows, width), lambda p, m: (0, p)),
        ),
        out_shape=jax.ShapeDtypeStruct((rows, 4 * width), BF),
        cost_estimate=pl.CostEstimate(flops=0, bytes_accessed=16 * rows * width, transcendentals=0),
    )(me.reshape(1), qkv_weight, out_weight)


def pick_ffn_kernel(me_ref, up, down, up_kept, down_kept):
    up_kept[...] = up[...]
    down_kept[...] = down[...]


def pick_ffn(me, up_weight, down_weight, reps, shards):
    rows, ff = up_weight.shape
    width = ff // (reps * shards)
    tall, dim = down_weight.shape[0] // reps, down_weight.shape[1]
    tile = dim // shards
    return pl.pallas_call(
        pick_ffn_kernel,
        grid_spec=pltpu.PrefetchScalarGridSpec(
            num_scalar_prefetch=1,
            grid=(shards,),
            in_specs=[
                pl.BlockSpec((rows, width), lambda p, m: (0, p * reps + m[0])),
                pl.BlockSpec((tall, tile), lambda p, m: (m[0], p)),
            ],
            out_specs=[
                pl.BlockSpec((rows, width), lambda p, m: (0, p)),
                pl.BlockSpec((tall, tile), lambda p, m: (0, p)),
            ],
        ),
        out_shape=[jax.ShapeDtypeStruct((rows, ff // reps), BF), jax.ShapeDtypeStruct((tall, dim), BF)],
        cost_estimate=pl.CostEstimate(flops=0, bytes_accessed=8 * rows * width * shards, transcendentals=0),
    )(me.reshape(1), up_weight, down_weight)


def place_cols_kernel(me_ref, own, ax, ay, low, high, out, parts):
    width = own.shape[1] // parts
    me = me_ref[0]
    t, tiles = pl.program_id(0), pl.num_programs(0)

    def put(k, piece):
        for p in range(parts):
            at = pl.multiple_of((p * 4 + (me ^ k)) * width, width)
            out[:, pl.ds(at, width)] = piece[:, p * width : (p + 1) * width].astype(out.dtype)

    put(0, own)
    put(1, ax)
    put(2, ay)

    @pl.when(t < tiles // 2)
    def _():
        put(3, low)

    @pl.when(t >= tiles // 2)
    def _():
        put(3, high)


def place_cols(me, pieces, parts, dtype=F32):
    cols = pieces[0].shape[1]
    rows = 2 * pieces[3].shape[0]
    tile = 64 if parts > 1 else 128
    half = rows // (2 * tile)
    full = pl.BlockSpec((tile, cols), lambda t, m: (t, 0))
    return pl.pallas_call(
        lambda *refs: place_cols_kernel(*refs, parts=parts),
        grid_spec=pltpu.PrefetchScalarGridSpec(
            num_scalar_prefetch=1,
            grid=(rows // tile,),
            in_specs=[
                full,
                full,
                full,
                pl.BlockSpec((tile, cols), lambda t, m: (jnp.minimum(t, half - 1), 0)),
                pl.BlockSpec((tile, cols), lambda t, m: (jnp.maximum(t - half, 0), 0)),
            ],
            out_specs=pl.BlockSpec((tile, 4 * cols), lambda t, m: (t, 0)),
        ),
        out_shape=jax.ShapeDtypeStruct((rows, 4 * cols), dtype),
        cost_estimate=pl.CostEstimate(flops=0, bytes_accessed=24 * rows * cols, transcendentals=0),
    )(me.reshape(1), *pieces)


def out_grad_kernel(me_ref, own, ax, ay, low, high, dt, small, joined):
    k = pl.program_id(0)
    per, tall, _ = joined.shape
    kept, rows, half = tall - PAD, dt.shape[0] // 4, low.shape[0]
    joined[:, kept:, :] = small[...]

    def heads(of, block):
        if of < 3:
            return (own, ax, ay)[of][block * rows : (block + 1) * rows, :]
        ref, at = (low, block * rows) if block * rows < half else (high, block * rows - half)
        return ref[at : at + rows, :]

    def put(of):
        grad = sum(mm_tn(heads(of, n ^ of), dt[n * rows : (n + 1) * rows, :]) for n in range(4)).astype(BF)
        for i in range(per):
            joined[i, :kept, :] = grad[i * kept : (i + 1) * kept, :]

    for of in range(4):
        pl.when(k == of)(lambda of=of: put(of))


def out_grad(me, pieces, dt, small):
    own, low = pieces[0], pieces[3]
    rows, cols = own.shape
    shards = small.shape[0]
    per = shards // 4
    tall = cols // per + PAD
    full = pl.BlockSpec((rows, cols), lambda k, m: (0, 0))
    part = pl.BlockSpec((low.shape[0], cols), lambda k, m: (0, 0))
    return pl.pallas_call(
        out_grad_kernel,
        grid_spec=pltpu.PrefetchScalarGridSpec(
            num_scalar_prefetch=1,
            grid=(4,),
            in_specs=[full, full, full, part, part]
            + [
                pl.BlockSpec((rows, cols), lambda k, m: (0, m[0])),
                pl.BlockSpec((per, PAD, cols), lambda k, m: (m[0] ^ k, 0, 0)),
            ],
            out_specs=pl.BlockSpec((per, tall, cols), lambda k, m: (m[0] ^ k, 0, 0)),
        ),
        out_shape=jax.ShapeDtypeStruct((shards, tall, cols), BF),
        compiler_params=pltpu.CompilerParams(vmem_limit_bytes=40 * 2**20),
        cost_estimate=pl.CostEstimate(flops=8 * rows * cols * cols, bytes_accessed=14 * rows * cols, transcendentals=0),
    )(me.reshape(1), *pieces, dt, small)


def place_rows_kernel(me_ref, own, ax, ay, low, high, out):
    k = pl.program_id(0)
    half = low.shape[0]

    @pl.when(k == 0)
    def _():
        out[...] = own[...].astype(out.dtype)

    @pl.when(k == 1)
    def _():
        out[...] = ax[...].astype(out.dtype)

    @pl.when(k == 2)
    def _():
        out[...] = ay[...].astype(out.dtype)

    @pl.when(k == 3)
    def _():
        out[:half] = low[...].astype(out.dtype)
        out[half:] = high[...].astype(out.dtype)


def place_rows(me, pieces, dtype=F32):
    own, low = pieces[0], pieces[3]
    rows, cols = own.shape
    full = pl.BlockSpec((rows, cols), lambda k, m: (0, 0))
    part = pl.BlockSpec((low.shape[0], cols), lambda k, m: (0, 0))
    return pl.pallas_call(
        place_rows_kernel,
        grid_spec=pltpu.PrefetchScalarGridSpec(
            num_scalar_prefetch=1,
            grid=(4,),
            in_specs=[full, full, full, part, part],
            out_specs=pl.BlockSpec((rows, cols), lambda k, m: (m[0] ^ k, 0)),
        ),
        out_shape=jax.ShapeDtypeStruct((4 * rows, cols), dtype),
        cost_estimate=pl.CostEstimate(flops=0, bytes_accessed=24 * rows * cols, transcendentals=0),
    )(me.reshape(1), *pieces)


def after(value, *deps):
    return lax.optimization_barrier((value,) + deps)[0]


def norm_forward(resid, gain, shift):
    center = resid - jnp.mean(resid, -1, keepdims=True)
    inv = lax.rsqrt(jnp.mean(center * center, -1, keepdims=True) + EPS)
    n = center * inv
    return n * gain + shift, n, inv


def norm_backward(g, gain, n, inv):
    dn = g * gain
    d = inv * (dn - jnp.mean(dn, -1, keepdims=True) - n * jnp.mean(dn * n, -1, keepdims=True))
    return d, jnp.sum(g * n, 0), jnp.sum(g, 0)


class Moves:
    def __init__(self, reps, shards):
        self.reps, self.shards = reps, shards
        self.square = reps == 4
        self.me = lax.axis_index("rep")
        self.xs = [(r, r ^ 1) for r in range(reps)]
        self.ys = [(r, r ^ 2) for r in range(reps)]
        self.ds = [(r, r ^ 3) for r in range(reps)]

    def over_x(self, a):
        return lax.ppermute(a, "rep", self.xs)

    def over_y(self, a):
        return lax.ppermute(a, "rep", self.ys)

    def gather_near(self, a):
        return a, self.over_x(a), self.over_y(a)

    def gather_far(self, near):
        own, ax, ay = near
        half = own.shape[0] // 32 * 16
        return [own, ax, ay, self.over_x(ay[:half]), self.over_y(ax[half:])]

    def gather_pieces(self, a, *meanwhile):
        near = self.gather_near(a)
        if meanwhile:
            near = lax.optimization_barrier(near + meanwhile)[:3]
        return self.gather_far(near)

    def gather_direct(self, a):
        half = a.shape[0] // 32 * 16
        both = self.over_both(a)
        return [a, self.over_x(a), self.over_y(a), both[:half], both[half:]]

    def gather_rows(self, a):
        if not self.square:
            return lax.all_gather(a, "rep", axis=0, tiled=True)
        return jnp.concatenate(self.gather_pieces(a), 0)

    def gather_small(self, a):
        if not self.square:
            return lax.all_gather(a, "rep", axis=0, tiled=True)
        return jnp.concatenate([a, self.over_x(a), self.over_y(a), lax.ppermute(a, "rep", self.ds)], 0)

    def scatter_sum(self, left, right, product, whole=False, between=None, first=()):
        rows = left.shape[0] // self.reps
        full = product(left, right) if whole or not self.square else None
        if not self.square:
            return lax.psum_scatter(full.astype(BF), "rep", scatter_dimension=0, tiled=True).astype(F32)
        cut = lambda a, k: a[k * rows : (k + 1) * rows]
        block = lambda a, k: cut(full, k) if whole else product(cut(a, k), right)
        half = rows // 2
        if whole:
            full = after(full, *first)
        far = block(left, 3).astype(BF)
        for_y, for_x = self.over_x(far[:half]), self.over_y(far[half:])
        left = after(left, far)
        px, py = block(left, 1), block(left, 2)
        px = jnp.concatenate([px[:half], px[half:] + for_x.astype(F32)], 0).astype(BF)
        py = jnp.concatenate([py[:half] + for_y.astype(F32), py[half:]], 0).astype(BF)
        got_x, got_y = self.over_x(px), self.over_y(py)
        own = block(left, 0)
        if between is not None:
            own = after(own, *between(px, py))
        return own + got_x.astype(F32) + got_y.astype(F32)

    def over_both(self, a):
        return lax.ppermute(a, "rep", self.ds)

    def swap_pieces(self, take):
        got = self.over_both(take(self.me ^ 3))
        half = got.shape[0] // 2
        return [take(self.me), self.over_x(take(self.me ^ 1)), self.over_y(take(self.me ^ 2)), got[:half], got[half:]]

    def swap(self, a):
        return lax.all_to_all(a, "rep", 0, 0, tiled=True)

    def gather_weight(self, w):
        return lax.all_gather(w, "fsdp", axis=0, tiled=True)

    def own_total(self, a):
        return lax.dynamic_index_in_dim(lax.psum(a, ("rep", "fsdp")), lax.axis_index("fsdp"), 0, False)

    def scatter_paired(self, g):
        shards = self.shards
        core = lax.axis_index("fsdp") % 2
        g = g.reshape(shards // 2, 2, g.shape[0] // shards, g.shape[1])
        take = lambda i: lax.dynamic_index_in_dim(g, i, 1, False)
        got = lax.ppermute(take(1 - core), "fsdp", [(i, i ^ 1) for i in range(shards)])
        both = (take(core).astype(F32) + got.astype(F32)).astype(BF).reshape(-1, g.shape[3])
        lines = [list(range(0, shards, 2)), list(range(1, shards, 2))]
        return lax.psum_scatter(both, "fsdp", scatter_dimension=0, axis_index_groups=lines, tiled=True)

    def scatter_weight(self, g):
        return lax.psum_scatter(g, "fsdp", scatter_dimension=0, tiled=True)


def per_device(
    tokens,
    lengths,
    cotangent,
    qkv_weight,
    qv_bias,
    out_weight,
    out_bias,
    attn_gain,
    attn_shift,
    up_weight,
    up_bias,
    down_weight,
    down_bias,
    ffn_gain,
    ffn_shift,
    reps,
    shards,
):
    mv = Moves(reps, shards)
    r = mv.me
    slots, seq, _ = tokens.shape
    rows = slots * seq
    ff = up_weight.shape[1]
    dr, fr = D // reps, ff // reps
    fpart = ff // (shards * reps)
    wrows = qkv_weight.shape[0]

    small = [qv_bias, out_bias, attn_gain, attn_shift, up_bias, down_bias, ffn_gain, ffn_shift]
    sizes = [s.shape[0] for s in small]
    packed = lax.all_gather(jnp.concatenate(small, 0), "fsdp", axis=0, tiled=False).astype(F32)
    full, at = [], 0
    for size in sizes:
        full.append(packed[:, at : at + size].reshape(-1))
        at += size
    b_qv, b_out, g_attn, s_attn, b_up, b_down, g_ffn, s_ffn = full
    bias_q = lax.dynamic_slice(b_qv, (r * dr,), (dr,))
    bias_v = lax.dynamic_slice(b_qv, (D + r * dr,), (dr,))
    bias_qkv = jnp.concatenate([bias_q, jnp.zeros_like(bias_q), bias_v], 0)
    bias_up = lax.dynamic_index_in_dim(b_up.reshape(shards, reps, fpart), r, 1, False).reshape(-1)

    fast = mv.square and fpart % 128 == 0
    if fast:
        attn_own = pick_attn(r, qkv_weight, out_weight, reps)
        up_own, down_own = pick_ffn(r, up_weight, down_weight, reps, shards)
        w_attn = mv.gather_weight(attn_own)
        w_qkv = w_attn[:, : 3 * dr]
        w_out = place_cols(r, mv.swap_pieces(lambda q: lax.dynamic_slice(w_attn, (q * dr, 3 * dr), (dr, dr))), 1, BF)
    else:
        pick_cols = lambda w, parts: lax.dynamic_index_in_dim(w.reshape(wrows, parts, reps, -1), r, 2, False).reshape(wrows, -1)
        up_own = pick_cols(up_weight, shards)
        down_own = lax.dynamic_slice(down_weight, (r * fpart, 0), (fpart, D))
        w_qkv = mv.gather_weight(pick_cols(qkv_weight, 3))
        w_out = mv.swap(mv.gather_weight(pick_cols(out_weight, 1)))
        w_out = w_out.reshape(reps, dr, dr).transpose(1, 0, 2).reshape(dr, D)
    w_up = mv.gather_weight(up_own)
    w_down = mv.gather_weight(down_own)

    x = tokens.reshape(rows, D)
    lens = mv.gather_small(lengths)
    x_all = mv.gather_rows(x)
    qkv = (mm(x_all, w_qkv) + bias_qkv).astype(BF)
    o = attn_fwd(lens, qkv, seq)
    attn = mv.scatter_sum(o, w_out, mm)
    x1, n1, inv1 = norm_forward(x.astype(F32) + attn + b_out, g_attn, s_attn)

    x1_all = mv.gather_rows(x1.astype(BF))
    hidden = mm(x1_all, w_up) + bias_up
    inner = 0.7978845608028654 * (hidden + 0.044715 * hidden * hidden * hidden)
    t = jnp.tanh(inner)
    act = (0.5 * hidden * (1.0 + t)).astype(BF)
    slope = 0.5 * (1.0 + t) + 0.5 * hidden * (1.0 - t * t) * (
        0.7978845608028654 * (1.0 + 3 * 0.044715 * hidden * hidden)
    )
    slope = slope.astype(BF)
    if fast:
        o_pieces = mv.gather_pieces(after(o, x1_all))
        act = after(act, *o_pieces)
    branch = mv.scatter_sum(act, w_down, mm)
    result, n2, inv2 = norm_forward(x1 + branch + b_down, g_ffn, s_ffn)
    output = result.astype(BF).reshape(slots, seq, D)

    valid = (jnp.arange(seq, dtype=jnp.int32)[None, :] < lengths[:, None]).astype(F32)
    g = cotangent.reshape(rows, D).astype(F32) * valid.reshape(rows, 1)
    dr2, d_gffn, d_sffn = norm_backward(g, g_ffn, n2, inv2)
    df = dr2.astype(BF)
    df_all = mv.gather_rows(df)
    d_wdown = mm_tn(act, df_all).astype(BF)
    df_all = after(df_all, d_wdown)
    d_wdown = mv.scatter_weight(d_wdown)
    d_bdown = jnp.sum(df.astype(F32), 0)
    dh, d_bup = hidden_grad(df_all, w_down, slope)
    def up_grad(*sent):
        return [mm_tn(x1_all, after(dh, *sent)).astype(BF)]

    kept = []

    def keep_up_grad(*sent):
        kept.extend(up_grad(*sent))
        return kept

    dx1 = dr2 + mv.scatter_sum(dh, w_up, mm_nt, True, keep_up_grad)
    d_wup = mv.scatter_weight((kept or up_grad())[0])

    dr1, d_gattn, d_sattn = norm_backward(dx1, g_attn, n1, inv1)
    dt = dr1.astype(BF)
    dt_all = after(mv.gather_rows(dt), d_wdown)
    d_bout = jnp.sum(dt.astype(F32), 0)
    do = mm_nt(dt_all, w_out).astype(BF)
    dqkv, sums = attn_bwd(lens, qkv, do, seq)
    if fast:
        down_near = mv.gather_near(after(d_wdown, dt_all))
        x_all = after(x_all, *down_near)
    d_wqkv = mm_tn(x_all, dqkv).astype(BF)
    if fast:
        dqkv = after(dqkv, d_wqkv)
        down_pieces = mv.gather_far(down_near)
    d_wqkv = mv.scatter_weight(d_wqkv)

    zero = jnp.zeros((2, D), F32)
    d_qv = lax.dynamic_update_slice(zero, jnp.stack([sums[0, :dr], sums[0, 2 * dr :]]), (0, r * dr)).reshape(-1)
    d_bup = lax.dynamic_update_slice(
        jnp.zeros((shards, reps, fpart), F32), d_bup.reshape(shards, 1, fpart), (0, r, 0)
    ).reshape(-1)
    grads = [d_qv, d_bout, d_gattn, d_sattn, d_bup, d_bdown, d_gffn, d_sffn]
    packed = jnp.concatenate([v.reshape(shards, -1) for v in grads], 1)
    if fast:
        small = packed.astype(BF).reshape(shards, -1, dr)
        small = jnp.pad(small, ((0, 0), (0, PAD - small.shape[1]), (0, 0)))
    else:
        packed = mv.own_total(packed)

    def late_grads(*sent):
        if fast:
            up_near = mv.gather_near(after(d_wup, *sent))
            placed = place_rows(r, after(down_pieces, *up_near))
            d_wout = out_grad(r, o_pieces, after(dt_all, *sent), small)
            kept.extend([d_wout.reshape(-1, dr), placed, up_near])
            return kept[:1]
        grad = mm_tn(after(o, *sent), dt_all).astype(BF)
        return [mv.swap(grad.reshape(dr, reps, dr).transpose(1, 0, 2).reshape(reps * dr, dr))]

    kept = []
    input_grad = dr1 + mv.scatter_sum(dqkv, w_qkv, mm_nt, True, late_grads, down_pieces if fast else ())
    d_wout = (kept or late_grads())[0]
    d_wout = mv.scatter_paired(d_wout) if fast else mv.scatter_weight(d_wout)
    input_grad = input_grad.reshape(slots, seq, D)

    if fast:
        d_wdown = kept[1]
        up_pieces = mv.gather_far(kept[2])
        d_wup = place_cols(r, up_pieces, shards)
        qkv_near = mv.gather_near(after(d_wqkv, *up_pieces))
        qkv_pieces = mv.gather_far(after(qkv_near, d_wup))
        out_pieces = mv.gather_direct(after(d_wout, d_wdown, input_grad, *qkv_pieces))
        d_wqkv = place_cols(r, qkv_pieces, 3)
        d_wout = place_cols(r, out_pieces, 1)
        below = [p[wrows:] for p in out_pieces[:3]] + [out_pieces[4][wrows - out_pieces[3].shape[0] :]]
        packed = sum(p.astype(F32) for p in below).reshape(-1)[: sum(sizes)]
    else:

        def spread(shard, parts):
            whole = lax.all_gather(shard, "rep", axis=0, tiled=False).astype(F32)
            whole = whole.reshape(reps, wrows, parts, -1).transpose(1, 2, 0, 3)
            return whole.reshape(wrows, -1)

        d_wdown = mv.gather_rows(d_wdown).astype(F32)
        d_wup, d_wout, d_wqkv = spread(d_wup, shards), spread(d_wout, 1), spread(d_wqkv, 3)

    pieces, at = [], 0
    for size in sizes:
        pieces.append(packed[at : at + size])
        at += size
    d_qv, d_bout, d_gattn, d_sattn, d_bup, d_bdown, d_gffn, d_sffn = pieces
    return (
        output,
        input_grad,
        d_wqkv,
        d_qv,
        d_wout,
        d_bout,
        d_gattn,
        d_sattn,
        d_wup,
        d_bup,
        d_wdown,
        d_bdown,
        d_gffn,
        d_sffn,
    )


def solution(mesh):
    reps, shards = mesh.shape["rep"], mesh.shape["fsdp"]
    seqs = P(("rep", "fsdp"), None, None)
    mat, vec = P("fsdp", None), P("fsdp")

    def program(*args):
        return per_device(*args, reps=reps, shards=shards)

    params = (mat, vec, mat, vec, vec, vec, mat, vec, mat, vec, vec, vec)
    return jax.shard_map(
        program,
        mesh=mesh,
        in_specs=(seqs, P(("rep", "fsdp")), seqs) + params,
        out_specs=(seqs, seqs) + params,
        check_vma=False,
    )
```
